128 devices in a mesh: ka: 64 (over z_lo, y, x, core), atoms: 2 (over z_hi).
Axes of the slice: x: 4, y: 4, z: 4 (z_hi: 2, z_lo: 2; z = z_hi * 2 + z_lo), core: 2. Of those that a mesh axis runs over, the one named last changes fastest.
Arguments:
- positions: float32 [64, 3, 65536], P('ka', None, 'atoms'), may hold values from 0 to 1
- counts: int32 [2, 3], P('atoms'), may hold values from 1 to 16384, 32768 in all within a row
- plan: int32 [8], replicated, may hold values from 0 to 63, as said below
- k_index: int32 [3, 8192], P(None, 'ka'), may hold values from -32 to 32, as said below
Outputs:
- factors: float32 [8, 6, 8192], P(None, None, 'ka')
The draws below stay inside these ranges and needn't reach their ends.
Inputs may be any that keep to these rules, and one draw needn't show every extreme that they name: `plan`: the frame slots are distinct. `counts`: each row sums to 32768. `k_index`: the 8192 k-vectors (columns) are distinct and none is the zero vector.
All inputs are finite; a program needn't handle non-finite values.
Results may differ from the reference program's by a relative error of at most 0.0003.
Values sent between devices are 32-bit elements; how exact they have to be, the bound alone decides.
A program may use at most 192 MiB of HBM per device.

```python
import math
import jax
import jax.numpy as jnp
import numpy as np
from jax import lax

A_DEV = 32768
KD = 128
FRAMES = 8
NAT = 65536
NK = 8192
SLOTS = 64
N_ATOMS = 2


def draw_plan(key, part):
    key = jax.random.fold_in(key, 7)
    middle_key, order_key = jax.random.split(key)
    middle = 1 + jax.random.permutation(middle_key, SLOTS - 2)[:FRAMES - 2]
    ordered = jnp.concatenate([jnp.zeros((1,), jnp.int32), middle.astype(jnp.int32), jnp.full((1,), SLOTS - 1, jnp.int32)])
    shuffle = jax.random.permutation(order_key, FRAMES)
    return ordered[shuffle].astype(jnp.int32)


def draw_k_index(key, part):
    key = jax.random.fold_in(key, 11)
    pick_key, order_key = jax.random.split(key)
    lattice_side = 65
    lattice_total = lattice_side * lattice_side * lattice_side
    middle_index = lattice_total // 2
    chosen = jax.random.permutation(pick_key, lattice_total - 3)[:NK - 2].astype(jnp.int32) + 1
    chosen = chosen + (chosen >= middle_index).astype(jnp.int32)
    corners = jnp.array([0, lattice_total - 1], dtype=jnp.int32)
    selected = jnp.concatenate([chosen, corners])
    selected = selected[jax.random.permutation(order_key, NK)]
    comp_first = selected // (lattice_side * lattice_side)
    comp_second = selected // lattice_side % lattice_side
    comp_third = selected % lattice_side
    return (jnp.stack([comp_first, comp_second, comp_third]) - 32).astype(jnp.int32)


def block_levels(own_key, shape, cuts, low, top_value):
    def one(dim, blocks):
        steps = jax.random.uniform(jax.random.fold_in(jax.random.fold_in(own_key, 6), dim), (blocks,), jnp.float32, low / len(cuts), top_value / len(cuts))
        return jnp.repeat(jnp.exp(steps), shape[dim] // blocks).reshape((-1,) + (1,) * (len(shape) - dim - 1))

    level = one(*cuts[0])
    for cut in cuts[1:]:
        level = level * one(*cut)
    return level


def split_up(amount, total, most, lean):
    weights = [(1 << 20) // math.isqrt(grade ** lean) + 1 for grade in range(2, amount + 1)]
    rest, holding = total - most - (amount - 1), [1] * (amount - 1)
    while rest > 0:
        candidates = [i for i in range(amount - 1) if holding[i] < most]
        mass, left = sum([weights[i] for i in candidates]), rest
        for i in candidates:
            addition = min(most - holding[i], max(1, left * weights[i] // mass), rest)
            holding[i] = holding[i] + addition
            rest = rest - addition
    return np.array([most] + holding)


def uneven_parts(key, number_of, total, most, slope):
    if number_of == 2:
        one = jax.random.randint(key, (), max(1, total - most), min(most, total - 1) + 1)
        return jnp.stack([one, total - one])
    lengths = jnp.asarray(split_up(number_of, total, most, slope), jnp.int32)
    twos = (number_of - 1) // 2
    source_of, sink = lengths[1:1 + 2 * twos:2], lengths[2:2 + 2 * twos:2]
    room = jnp.minimum(source_of - 1, most - sink)
    passed = jax.random.randint(jax.random.fold_in(key, 1), (twos,), 0, 1 << 20) % (room + 1)
    lengths = lengths.at[1:1 + 2 * twos:2].set(source_of - passed).at[2:2 + 2 * twos:2].set(sink + passed)
    return lengths[jax.random.permutation(jax.random.fold_in(key, 2), number_of)]


def setup_inputs(seed: int = 0) -> dict:
    keys = jax.random.split(jax.random.key(seed), 5)
    return {
        "positions": jnp.clip(1.0 * jax.random.uniform(keys[0], (SLOTS, 3, NAT), jnp.float32) ** block_levels(keys[0], (SLOTS, 3, NAT), ((0, 64), (2, 2)), -0.2, 0.2), 0.0, 1.0),
        "counts": jax.vmap(lambda own: uneven_parts(own, 3, A_DEV, A_DEV // 2, 1))(jax.random.split(keys[1], N_ATOMS)).reshape((N_ATOMS, 3)).astype(jnp.int32),
        "plan": draw_plan(jax.random.fold_in(keys[4], 71), 0),
        "k_index": draw_k_index(jax.random.fold_in(keys[4], 71), 0),
    }


def species_member(counts):
    atom_index = jnp.arange(A_DEV, dtype=jnp.int32)
    run_ends = jnp.cumsum(counts, axis=1)
    run_starts = run_ends - counts
    inside = (atom_index[None, None, :] >= run_starts[:, :, None]) & (atom_index[None, None, :] < run_ends[:, :, None])
    member = inside.astype(jnp.float32)
    return jnp.transpose(member, (1, 0, 2)).reshape(3, -1)


def block_modes(coords, member, k_block):
    k_float = k_block.astype(jnp.float32)
    phase = k_float[0][:, None] * coords[0][None, :] + k_float[1][:, None] * coords[1][None, :]
    phase = (phase + k_float[2][:, None] * coords[2][None, :]) * (2.0 * math.pi)
    cosines = jnp.cos(phase)
    sines = jnp.sin(phase)
    dims = (((1,), (1,)), ((), ()))
    cos_part = lax.dot_general(member, cosines, dims, precision=lax.Precision.HIGHEST, preferred_element_type=jnp.float32)
    sin_part = lax.dot_general(member, sines, dims, precision=lax.Precision.HIGHEST, preferred_element_type=jnp.float32)
    return jnp.stack([cos_part, sin_part])


def transform(window_modes, total_atoms):
    frame_count = window_modes.shape[0]
    steps_index = jnp.arange(frame_count, dtype=jnp.float32)
    angles = steps_index[:, None] * steps_index[None, :] * (2.0 * math.pi / frame_count)
    cos_table = jnp.cos(angles)
    sin_table = jnp.sin(angles)
    cos_modes = window_modes[:, 0]
    sin_modes = window_modes[:, 1]
    high = lax.Precision.HIGHEST
    real_part = jnp.einsum("ft,tsk->fsk", cos_table, cos_modes, precision=high) + jnp.einsum("ft,tsk->fsk", sin_table, sin_modes, precision=high)
    imag_part = jnp.einsum("ft,tsk->fsk", cos_table, sin_modes, precision=high) - jnp.einsum("ft,tsk->fsk", sin_table, cos_modes, precision=high)
    first_species = jnp.array([0, 0, 0, 1, 1, 2], dtype=jnp.int32)
    second_species = jnp.array([0, 1, 2, 1, 2, 2], dtype=jnp.int32)
    product = real_part[:, first_species] * real_part[:, second_species] + imag_part[:, first_species] * imag_part[:, second_species]
    return product / (frame_count * total_atoms)


def reference(positions, counts, plan, k_index):
    member = species_member(counts)
    k_blocks = jnp.transpose(k_index.reshape(3, NK // KD, KD), (1, 0, 2))
    frame_list = []
    for frame in range(FRAMES):
        coords = lax.dynamic_index_in_dim(positions, plan[frame], 0, keepdims=False)
        per_block = lax.map(lambda k_block: block_modes(coords, member, k_block), k_blocks)
        frame_list.append(jnp.transpose(per_block, (1, 2, 0, 3)).reshape(2, 3, NK))
    window_modes = jnp.stack(frame_list)
    return transform(window_modes, NAT)
```

```python
import jax, jax.numpy as jnp, numpy as np
from jax import lax
from jax.sharding import PartitionSpec as P
from jax.experimental import pallas as pl
from jax.experimental.pallas import tpu as pltpu

LINES = 88
COARSE = 13
CHUNK = 256
f32 = jnp.float32
bf16 = jnp.bfloat16

def fit_coefs():
    t = np.cos(np.pi * (np.arange(4000) + 0.5) / 4000) * 0.5
    u = t * t
    a = np.vander(u, 6, increasing=True)
    ps = np.linalg.lstsq(a * t[:, None], np.sin(np.pi * t), rcond=None)[0]
    pc = np.linalg.lstsq(a, np.cos(np.pi * t), rcond=None)[0]
    return [float(x) for x in ps], [float(x) for x in pc]

SIN_C, COS_C = fit_coefs()

def waves(cycles):
    t = cycles - jnp.round(cycles)
    u = t * t
    s = jnp.full_like(u, SIN_C[-1])
    for c in SIN_C[-2::-1]:
        s = s * u + c
    s = s * t
    q = jnp.full_like(u, COS_C[-1])
    for c in COS_C[-2::-1]:
        q = q * u + c
    twice = s + s
    return 1.0 - twice * s, twice * q

def split(x):
    hi = x.astype(bf16)
    lo = (x - hi.astype(f32)).astype(bf16)
    return hi, lo

def balanced(index, base, reach, mul, shift, below=0):
    upper = (((index + reach + base * below) * mul) >> shift) - below
    return upper, index - base * upper

def modes_kernel(counts, starts, pick_tile, pick_shift, x_ref, sign_ref, out_ref, e01, e2, fine, rhs, acc, grid):
    acc[...] = jnp.zeros_like(acc)
    ends = [counts[0]]
    for s in range(1, 3):
        ends.append(ends[-1] + counts[s])
    lane = lax.broadcasted_iota(jnp.int32, (1, CHUNK), 1)

    line = lax.broadcasted_iota(jnp.int32, (LINES, CHUNK), 0)
    q0, q1 = balanced(line, 13, 6, 79, 10)
    q0 = (5 * q0).astype(f32)
    q1 = (5 * q1).astype(f32)
    col = lax.broadcasted_iota(jnp.int32, (64, CHUNK), 0)
    r0, rest = balanced(col, 25, 12, 41, 10)
    r1, r2 = balanced(rest, 5, 2, 205, 10, 3)

    def chunk_step(i, _):
        off = pl.multiple_of(i * CHUNK, CHUNK)
        xs = [x_ref[d:d + 1, pl.ds(off, CHUNK)] for d in range(3)]
        xs = [x - jnp.round(x) for x in xs]
        c, s_ = waves(q0 * xs[0] + q1 * xs[1])
        e01[0:LINES] = c
        e01[LINES:2 * LINES] = s_
        depth = lax.broadcasted_iota(jnp.int32, (8, CHUNK), 0)
        c, s_ = waves((5 * depth).astype(f32) * xs[2])
        e2[0:8] = c
        e2[8:16] = s_
        c, s_ = waves(r0.astype(f32) * xs[0] + r1.astype(f32) * xs[1] + r2.astype(f32) * xs[2])
        fine[0:64] = c
        fine[64:128] = s_
        first = starts[i // (512 // CHUNK)] + lax.rem(i, 512 // CHUNK) * CHUNK

        def species_step(sp, _):
            end = jnp.where(sp == 0, ends[0], jnp.where(sp == 1, ends[1], ends[2]))
            begin = end - counts[sp]

            @pl.when(jnp.logical_and(begin < first + CHUNK, end > first))
            def _():
                where = lane + first
                mask = jnp.logical_and(where >= begin, where < end).astype(f32)
                hi, lo = split(fine[...] * mask)
                rhs[0:128, 0:CHUNK] = hi
                rhs[128:256, 0:CHUNK] = lo
                rhs[0:128, CHUNK:] = hi
                rhs[128:256, CHUNK:] = lo

                def depth_step(l, _):
                    row = jnp.where(l < 7, l, l + 2)
                    wave = e01[...] * e2[pl.ds(row, 1)]
                    hi, lo = split(wave)
                    lhs = jnp.concatenate([hi, lo], axis=1)
                    acc[sp, l] += lax.dot_general(lhs, rhs[...], (((1,), (1,)), ((), ())), preferred_element_type=f32)
                    return 0

                lax.fori_loop(0, COARSE, depth_step, 0, unroll=True)
            return 0
        lax.fori_loop(0, 3, species_step, 0)
        return 0

    lax.fori_loop(0, x_ref.shape[1] // CHUNK, chunk_step, 0)

    def halves(sp, l, part):
        rows = acc[sp, l, pl.ds(part * LINES, LINES), :]
        return rows[:, :128] + rows[:, 128:]

    def put(q2, sp, part, value):
        grid[pl.ds((q2 + 6) * LINES * 8 + part * 4 + sp, LINES, stride=8), :] = value

    for sp in range(3):
        put(0, sp, 0, halves(sp, 0, 0))
        put(0, sp, 1, halves(sp, 0, 1))
        for l in range(1, 7):
            cc, sc = halves(sp, l, 0), halves(sp, l, 1)
            cs, ss = halves(sp, l + 6, 0), halves(sp, l + 6, 1)
            put(l, sp, 0, cc - ss)
            put(-l, sp, 0, cc + ss)
            put(l, sp, 1, sc + cs)
            put(-l, sp, 1, sc - cs)

    lanes = lax.broadcasted_iota(jnp.int32, (8, 128), 1)

    def block_step(b, _):
        at_c = jnp.zeros((8, 128), f32)
        at_s = jnp.zeros((8, 128), f32)
        for j in range(128):
            row = pl.multiple_of(pick_tile[b, j], 8)
            tile = pltpu.roll(grid[pl.ds(row, 8), :], pick_shift[b, j], axis=1)
            at_c = jnp.where(lanes == j, tile, at_c)
            at_s = jnp.where(lanes == (j + 64) % 128, tile, at_s)
        at_s = pltpu.roll(at_s, 64, axis=1)
        sq = sign_ref[b, 0:1]
        sr = sign_ref[b, 1:2]
        real = at_c - sq * sr * pltpu.roll(at_s, 4, axis=0)
        imag = sq * at_c + sr * pltpu.roll(at_s, 4, axis=0)
        sub = lax.broadcasted_iota(jnp.int32, (8, 128), 0)
        out_ref[b] = jnp.where(sub < 4, real, imag)
        return 0

    lax.fori_loop(0, 64, block_step, 0)

def picks(k_index):
    n = k_index + 32
    q = ((n * 205) >> 10) - 6
    r = k_index - 5 * q
    jc = 13 * q[0] + q[1]
    sq = jnp.where(jc < 0, -1, 1)
    tile = (sq * q[2] + 6) * LINES + jnp.abs(jc)
    rc = 25 * r[0] + 5 * r[1] + r[2]
    sr = jnp.where(rc < 0, -1, 1)
    lane = jnp.arange(k_index.shape[1], dtype=jnp.int32) & 127
    shift = (lane - jnp.abs(rc)) & 127
    return tile * 8, shift, sq, sr

def call_modes(counts, starts, tiles, shifts, x, signs, interpret=False):
    smem = pl.BlockSpec(memory_space=pltpu.SMEM)
    vmem = pl.BlockSpec(memory_space=pltpu.VMEM)
    return pl.pallas_call(
        modes_kernel,
        out_shape=jax.ShapeDtypeStruct((64, 8, 128), f32),
        in_specs=[smem, smem, smem, smem, vmem, vmem],
        out_specs=vmem,
        scratch_shapes=[
            pltpu.VMEM((2 * LINES, CHUNK), f32),
            pltpu.VMEM((16, CHUNK), f32),
            pltpu.VMEM((128, CHUNK), f32),
            pltpu.VMEM((256, 2 * CHUNK), bf16),
            pltpu.VMEM((3, COARSE, 2 * LINES, 256), f32),
            pltpu.VMEM((13 * LINES * 8, 128), f32),
        ],
        compiler_params=pltpu.CompilerParams(vmem_limit_bytes=56 * 1024 * 1024),
        interpret=interpret,
    )(counts, starts, tiles, shifts, x, signs)


def transform(window, total_atoms):
    frames = window.shape[0]
    turn = np.arange(frames)[:, None] * np.arange(frames)[None, :] % frames
    cos_table = jnp.asarray(np.cos(2 * np.pi * turn / frames), f32)[:, :, None, None]
    sin_table = jnp.asarray(np.sin(2 * np.pi * turn / frames), f32)[:, :, None, None]
    c, s = window[None, :, 0:3], window[None, :, 4:7]
    real = jnp.sum(cos_table * c + sin_table * s, axis=1)
    imag = jnp.sum(cos_table * s - sin_table * c, axis=1)
    pairs = ((0, 0), (0, 1), (0, 2), (1, 1), (1, 2), (2, 2))
    out = [real[:, a] * real[:, b] + imag[:, a] * imag[:, b] for a, b in pairs]
    return jnp.stack(out, axis=1) / (frames * total_atoms)


def local(positions, counts, plan, k_index):
    atoms_here = positions.shape[2]
    devices = lax.axis_size("ka")
    piece = atoms_here // devices
    me = lax.axis_index("ka")
    pieces = jnp.transpose(positions[0].reshape(3, devices, piece), (1, 0, 2))
    slots = lax.all_to_all(pieces, "ka", 0, 0, tiled=True)
    window = slots[plan]
    groups = [[high * 16 + f * 2 + core for f in range(8)] for high in range(4) for core in range(2)]
    own = lax.all_to_all(window, "ka", 0, 0, axis_index_groups=groups, tiled=True)
    x = jnp.transpose(own, (1, 0, 2)).reshape(3, 8 * piece)
    starts = (me // 16 * 16 + jnp.arange(8, dtype=jnp.int32) * 2 + lax.rem(me, 2)) * piece
    tile, shift, sq, sr = picks(k_index)
    meta = lax.all_gather(jnp.stack([tile, shift, sq, sr]), "ka")
    modes = call_modes(counts[0], starts.astype(jnp.int32), meta[:, 0], meta[:, 1], x, meta[:, 2:].astype(f32))
    parts = lax.all_to_all(modes, "ka", 0, 0, tiled=True)
    total = jnp.sum(parts.reshape(4, 8, 2, 8, 128), axis=(0, 2))
    total = lax.psum(total, "atoms")
    return transform(total, atoms_here * lax.axis_size("atoms"))


def solution(mesh):
    return jax.shard_map(
        local,
        mesh=mesh,
        in_specs=(P("ka", None, "atoms"), P("atoms", None), P(), P(None, "ka")),
        out_specs=P(None, None, "ka"),
        check_vma=False,
    )
```

```python
import functools
import math

import jax
import jax.numpy as jnp
import numpy as np
from jax import lax
from jax.experimental import pallas as pl
from jax.experimental.pallas import tpu as pltpu
from jax.sharding import PartitionSpec as P

MESH = pl.DeviceIdType.MESH
FRAMES = 8
LINES = 88
COARSE = 13
CHUNK = 256
f32 = jnp.float32
bf16 = jnp.bfloat16

def fit_coefs():
    t = np.cos(np.pi * (np.arange(4000) + 0.5) / 4000) * 0.5
    u = t * t
    a = np.vander(u, 6, increasing=True)
    ps = np.linalg.lstsq(a * t[:, None], np.sin(np.pi * t), rcond=None)[0]
    pc = np.linalg.lstsq(a, np.cos(np.pi * t), rcond=None)[0]
    return [float(x) for x in ps], [float(x) for x in pc]

SIN_C, COS_C = fit_coefs()

def waves(cycles):
    t = cycles - jnp.round(cycles)
    u = t * t
    s = jnp.full_like(u, SIN_C[-1])
    for c in SIN_C[-2::-1]:
        s = s * u + c
    s = s * t
    q = jnp.full_like(u, COS_C[-1])
    for c in COS_C[-2::-1]:
        q = q * u + c
    twice = s + s
    return 1.0 - twice * s, twice * q

def split(x):
    hi = x.astype(bf16)
    lo = (x - hi.astype(f32)).astype(bf16)
    return hi, lo

def balanced(index, base, reach, mul, shift, below=0):
    upper = (((index + reach + base * below) * mul) >> shift) - below
    return upper, index - base * upper

def modes_kernel(counts, base, x_ref, word_ref, out_ref, e01, e2, fine, rhs, acc, grid, pick, pick_sem):
    piece = x_ref.shape[2] * 128
    per_piece = piece // CHUNK
    fetch = pltpu.make_async_copy(word_ref, pick, pick_sem)
    fetch.start()
    acc[...] = jnp.zeros_like(acc)
    ends = [counts[0, 0]]
    for s in range(1, 3):
        ends.append(ends[-1] + counts[0, s])
    lane = lax.broadcasted_iota(jnp.int32, (1, CHUNK), 1)

    line = lax.broadcasted_iota(jnp.int32, (LINES, CHUNK), 0)
    q0, q1 = balanced(line, 13, 6, 79, 10)
    q0 = (5 * q0).astype(f32)
    q1 = (5 * q1).astype(f32)
    col = lax.broadcasted_iota(jnp.int32, (64, CHUNK), 0)
    r0, rest = balanced(col, 25, 12, 41, 10)
    r1, r2 = balanced(rest, 5, 2, 205, 10, 3)

    def chunk_step(i, _):
        off = lax.rem(i, per_piece) * CHUNK
        xs = []
        for d in range(3):
            rows = [x_ref[i // per_piece, d, pl.ds(lax.rem(i, per_piece) * (CHUNK // 128) + n, 1)] for n in range(CHUNK // 128)]
            xs.append(jnp.concatenate(rows, axis=1))
        xs = [x - jnp.round(x) for x in xs]
        c, s_ = waves(q0 * xs[0] + q1 * xs[1])
        e01[0:LINES] = c
        e01[LINES:2 * LINES] = s_
        depth = lax.broadcasted_iota(jnp.int32, (8, CHUNK), 0)
        c, s_ = waves((5 * depth).astype(f32) * xs[2])
        e2[0:8] = c
        e2[8:16] = s_
        c, s_ = waves(r0.astype(f32) * xs[0] + r1.astype(f32) * xs[1] + r2.astype(f32) * xs[2])
        fine[0:64] = c
        fine[64:128] = s_
        first = (base[0] + 2 * (i // per_piece)) * piece + off

        def species_step(sp, _):
            end = jnp.where(sp == 0, ends[0], jnp.where(sp == 1, ends[1], ends[2]))
            begin = end - counts[0, sp]

            @pl.when(jnp.logical_and(begin < first + CHUNK, end > first))
            def _():
                where = lane + first
                mask = jnp.logical_and(where >= begin, where < end).astype(f32)
                hi, lo = split(fine[...] * mask)
                rhs[0:128, 0:CHUNK] = hi
                rhs[128:256, 0:CHUNK] = lo
                rhs[0:128, CHUNK:] = hi
                rhs[128:256, CHUNK:] = lo

                def depth_step(l, _):
                    row = jnp.where(l < 7, l, l + 2)
                    wave = e01[...] * e2[pl.ds(row, 1)]
                    hi, lo = split(wave)
                    lhs = jnp.concatenate([hi, lo], axis=1)
                    acc[sp, l] += lax.dot_general(lhs, rhs[...], (((1,), (1,)), ((), ())), preferred_element_type=f32)
                    return 0

                lax.fori_loop(0, COARSE, depth_step, 0, unroll=True)
            return 0
        lax.fori_loop(0, 3, species_step, 0)
        return 0

    lax.fori_loop(0, FRAMES * per_piece, chunk_step, 0)

    def halves(sp, l, part):
        rows = acc[sp, l, pl.ds(part * LINES, LINES), :]
        return rows[:, :128] + rows[:, 128:]

    def put(q2, sp, part, value):
        grid[pl.ds((q2 + 6) * LINES * 8 + part * 4 + sp, LINES, stride=8), :] = value

    for sp in range(3):
        put(0, sp, 0, halves(sp, 0, 0))
        put(0, sp, 1, halves(sp, 0, 1))
        for l in range(1, 7):
            cc, sc = halves(sp, l, 0), halves(sp, l, 1)
            cs, ss = halves(sp, l + 6, 0), halves(sp, l + 6, 1)
            put(l, sp, 0, cc - ss)
            put(-l, sp, 0, cc + ss)
            put(l, sp, 1, sc + cs)
            put(-l, sp, 1, sc - cs)

    lanes = lax.broadcasted_iota(jnp.int32, (8, 128), 1)

    fetch.wait()

    def block_step(b, _):
        at_c = jnp.zeros((8, 128), f32)
        at_s = jnp.zeros((8, 128), f32)
        for j in range(128):
            word = pick[b, 0, j]
            row = pl.multiple_of((word >> 9) * 8, 8)
            tile = pltpu.roll(grid[pl.ds(row, 8), :], word & 127, axis=1)
            at_c = jnp.where(lanes == j, tile, at_c)
            at_s = jnp.where(lanes == (j + 64) % 128, tile, at_s)
        at_s = pltpu.roll(at_s, 64, axis=1)
        word = word_ref[b]
        sq = jnp.where(((word >> 7) & 1) > 0, -1.0, 1.0)
        sr = jnp.where(((word >> 8) & 1) > 0, -1.0, 1.0)
        real = at_c - sq * sr * pltpu.roll(at_s, 4, axis=0)
        imag = sq * at_c + sr * pltpu.roll(at_s, 4, axis=0)
        sub = lax.broadcasted_iota(jnp.int32, (8, 128), 0)
        out_ref[b] = jnp.where(sub < 4, real, imag)
        return 0

    lax.fori_loop(0, 64, block_step, 0)

def picks(k_index):
    n = [k_index[d:d + 1] for d in range(3)]
    q, r = zip(*[balanced(v, 5, 2, 205, 10, 6) for v in n])
    jc = 13 * q[0] + q[1]
    sq = jnp.where(jc < 0, 1, 0)
    tile = (jnp.where(jc < 0, -q[2], q[2]) + 6) * LINES + jnp.abs(jc)
    rc = 25 * r[0] + 5 * r[1] + r[2]
    sr = jnp.where(rc < 0, 1, 0)
    lane = lax.broadcasted_iota(jnp.int32, rc.shape, 1)
    shift = (lane - jnp.abs(rc)) & 127
    return tile * 512 + sr * 256 + sq * 128 + shift


def call_modes(counts, base, x, words):
    smem = pl.BlockSpec(memory_space=pltpu.SMEM)
    vmem = pl.BlockSpec(memory_space=pltpu.VMEM)
    return pl.pallas_call(
        modes_kernel,
        out_shape=jax.ShapeDtypeStruct((64, 8, 128), f32),
        in_specs=[smem, smem, vmem, vmem],
        out_specs=vmem,
        scratch_shapes=[
            pltpu.VMEM((2 * LINES, CHUNK), f32),
            pltpu.VMEM((16, CHUNK), f32),
            pltpu.VMEM((128, CHUNK), f32),
            pltpu.VMEM((256, 2 * CHUNK), bf16),
            pltpu.VMEM((3, COARSE, 2 * LINES, 256), f32),
            pltpu.VMEM((13 * LINES * 8, 128), f32),
            pltpu.SMEM(words.shape, jnp.int32),
            pltpu.SemaphoreType.DMA,
        ],
        compiler_params=pltpu.CompilerParams(vmem_limit_bytes=20 * 1024 * 1024),
    )(counts, base, x, words)


def spread_kernel(plan, k_ref, pos_ref, x_ref, word_ref, slots, stage, word, send_sem, recv_sem, own_sem):
    me = lax.axis_index("ka")
    count = lax.axis_size("ka")
    rows = slots.shape[2]
    barrier = pltpu.get_barrier_semaphore()

    def greet(i, _):
        pl.semaphore_signal(barrier, inc=1, device_id={"ka": lax.rem(me + i, count)}, device_id_type=MESH)
        return 0

    lax.fori_loop(1, count, greet, 0)
    word[...] = picks(k_ref[...])
    pl.semaphore_wait(barrier, count - 1)

    def send(i, _):
        to = lax.rem(me + i, count)
        pltpu.make_async_remote_copy(
            src_ref=pos_ref.at[:, pl.ds(to * rows, rows)],
            dst_ref=slots.at[me],
            send_sem=send_sem.at[0],
            recv_sem=recv_sem.at[0],
            device_id={"ka": to},
            device_id_type=MESH,
        ).start()
        return 0

    lax.fori_loop(1, count, send, 0)
    keep = pltpu.make_async_copy(pos_ref.at[:, pl.ds(me * rows, rows)], slots.at[me], own_sem)
    keep.start()

    def send_word(i, _):
        pltpu.make_async_remote_copy(
            src_ref=word,
            dst_ref=word_ref.at[me],
            send_sem=send_sem.at[1],
            recv_sem=recv_sem.at[1],
            device_id={"ka": lax.rem(me + i, count)},
            device_id_type=MESH,
        ).start()
        return 0

    lax.fori_loop(1, count, send_word, 0)
    word_ref[me] = word[...]
    keep.wait()
    most = slots.at[pl.ds(0, count - 1)]
    pltpu.make_async_copy(most, most, recv_sem.at[0]).wait()
    frame = lax.rem(me // 2, FRAMES)
    base = me - 2 * frame
    for f in range(FRAMES):
        stage[f] = slots[plan[f]]

    def hand_on(i, _):
        to = lax.rem(frame + i, FRAMES)
        pltpu.make_async_remote_copy(
            src_ref=stage.at[to],
            dst_ref=x_ref.at[frame],
            send_sem=send_sem.at[2],
            recv_sem=recv_sem.at[2],
            device_id={"ka": base + 2 * to},
            device_id_type=MESH,
        ).start()
        return 0

    lax.fori_loop(1, FRAMES, hand_on, 0)
    x_ref[frame] = stage[frame]
    words = word_ref.at[pl.ds(0, count - 1)]
    pltpu.make_async_copy(words, words, recv_sem.at[1]).wait()
    rest = x_ref.at[pl.ds(0, FRAMES - 1)]
    pltpu.make_async_copy(rest, rest, recv_sem.at[2]).wait()
    pltpu.make_async_copy(most, most, send_sem.at[0]).wait()
    pltpu.make_async_copy(words, words, send_sem.at[1]).wait()
    pltpu.make_async_copy(rest, rest, send_sem.at[2]).wait()


def call_spread(plan, k_index, positions):
    smem = pl.BlockSpec(memory_space=pltpu.SMEM)
    vmem = pl.BlockSpec(memory_space=pltpu.VMEM)
    count = lax.axis_size("ka")
    rows = positions.shape[2] // (128 * count)
    positions = positions.reshape(3, rows * count, 128)
    return pl.pallas_call(
        spread_kernel,
        out_shape=(
            jax.ShapeDtypeStruct((FRAMES, 3, rows, 128), f32),
            jax.ShapeDtypeStruct((count, 1, k_index.shape[1]), jnp.int32),
        ),
        in_specs=[smem, vmem, pl.BlockSpec(memory_space=pl.ANY)],
        out_specs=(vmem, vmem),
        scratch_shapes=[
            pltpu.VMEM((count, 3, rows, 128), f32),
            pltpu.VMEM((FRAMES, 3, rows, 128), f32),
            pltpu.VMEM((1, k_index.shape[1]), jnp.int32),
            pltpu.SemaphoreType.DMA((3,)),
            pltpu.SemaphoreType.DMA((3,)),
            pltpu.SemaphoreType.DMA,
        ],
        compiler_params=pltpu.CompilerParams(collective_id=0, has_side_effects=True),
    )(plan, k_index, positions)


def factors_kernel(scale, modes_ref, out_ref, parts, send_sem, recv_sem, own_sem):
    me = lax.axis_index("ka")
    half = lax.axis_index("atoms")
    count = lax.axis_size("ka")
    barrier = pltpu.get_barrier_semaphore()

    def greet(i, _):
        for h in range(2):
            @pl.when(i + h > 0)
            def _():
                pl.semaphore_signal(
                    barrier, inc=1, device_id={"ka": lax.rem(me + i, count), "atoms": lax.rem(half + h, 2)},
                    device_id_type=MESH)
        return 0

    lax.fori_loop(0, count, greet, 0)
    pl.semaphore_wait(barrier, 2 * count - 1)
    slot = half * count + me

    def send(i, _):
        to = lax.rem(me + i, count)
        for h in range(2):
            @pl.when(i + h > 0)
            def _():
                pltpu.make_async_remote_copy(
                    src_ref=modes_ref.at[to],
                    dst_ref=parts.at[slot],
                    send_sem=send_sem,
                    recv_sem=recv_sem,
                    device_id={"ka": to, "atoms": lax.rem(half + h, 2)},
                    device_id_type=MESH,
                ).start()
        return 0

    lax.fori_loop(0, count, send, 0)
    keep = pltpu.make_async_copy(modes_ref.at[me], parts.at[slot], own_sem)
    keep.start()
    keep.wait()
    most = parts.at[pl.ds(0, 2 * count - 1)]
    pltpu.make_async_copy(most, most, recv_sem).wait()
    window = []
    for f in range(FRAMES):
        total = None
        for high in range(2 * count // 16):
            for core in range(2):
                part = parts[high * 16 + f * 2 + core]
                total = part if total is None else total + part
        window.append(total)
    upper = lax.broadcasted_iota(jnp.int32, (8, 128), 0) < 4
    crossed = [jnp.where(upper, 1.0, -1.0) * pltpu.roll(w, 4, axis=0) for w in window]
    pairs = ((0, 0), (0, 1), (0, 2), (1, 1), (1, 2), (2, 2))
    for f in range(FRAMES):
        wave = window[0]
        for t in range(1, FRAMES):
            turn = 2 * math.pi * (f * t % FRAMES) / FRAMES
            wave = wave + math.cos(turn) * window[t] + math.sin(turn) * crossed[t]
        for p, (a, b) in enumerate(pairs):
            value = wave[a:a + 1] * wave[b:b + 1] + wave[4 + a:5 + a] * wave[4 + b:5 + b]
            out_ref[f, p:p + 1] = value * scale
    pltpu.make_async_copy(most, most, send_sem).wait()


def call_factors(modes, total_atoms):
    vmem = pl.BlockSpec(memory_space=pltpu.VMEM)
    count = lax.axis_size("ka")
    return pl.pallas_call(
        functools.partial(factors_kernel, 1.0 / (FRAMES * total_atoms)),
        out_shape=jax.ShapeDtypeStruct((FRAMES, 6, modes.shape[2]), f32),
        in_specs=[vmem],
        out_specs=vmem,
        scratch_shapes=[
            pltpu.VMEM((2 * count, 8, modes.shape[2]), f32),
            pltpu.SemaphoreType.DMA,
            pltpu.SemaphoreType.DMA,
            pltpu.SemaphoreType.DMA,
        ],
        compiler_params=pltpu.CompilerParams(collective_id=1, has_side_effects=True),
    )(modes)


def local(positions, counts, plan, k_index):
    me = lax.axis_index("ka")
    x, words = call_spread(plan, k_index, positions)
    first = me - lax.rem(me // 2, FRAMES) * 2
    modes = call_modes(counts, first.astype(jnp.int32).reshape(1), x, words)
    return call_factors(modes, positions.shape[2] * lax.axis_size("atoms"))


def solution(mesh):
    return jax.shard_map(
        local,
        mesh=mesh,
        in_specs=(P("ka", None, "atoms"), P("atoms", None), P(), P(None, "ka")),
        out_specs=P(None, None, "ka"),
        check_vma=False,
    )
```

```python
import functools
import math

import jax
import jax.numpy as jnp
import numpy as np
from jax import lax
from jax.experimental import pallas as pl
from jax.experimental.pallas import tpu as pltpu
from jax.sharding import PartitionSpec as P

MESH = pl.DeviceIdType.MESH
FRAMES = 8
LINES = 88
COARSE = 13
CHUNK = 256
GROUP = 4
f32 = jnp.float32
bf16 = jnp.bfloat16

def fit_coefs():
    t = np.cos(np.pi * (np.arange(4000) + 0.5) / 4000) * 0.5
    u = t * t
    a = np.vander(u, 5, increasing=True)
    ps = np.linalg.lstsq(a * t[:, None], np.sin(np.pi * t), rcond=None)[0]
    pc = np.linalg.lstsq(a, np.cos(np.pi * t), rcond=None)[0]
    return [float(x) for x in ps], [float(x) for x in pc]

SIN_C, COS_C = fit_coefs()

def waves(cycles):
    t = cycles - jnp.round(cycles)
    u = t * t
    s = jnp.full_like(u, SIN_C[-1])
    for c in SIN_C[-2::-1]:
        s = s * u + c
    s = s * t
    q = jnp.full_like(u, COS_C[-1])
    for c in COS_C[-2::-1]:
        q = q * u + c
    twice = s + s
    return 1.0 - twice * s, twice * q

def split(x):
    hi = x.astype(bf16)
    lo = (x - hi.astype(f32)).astype(bf16)
    return hi, lo

def balanced(index, base, reach, mul, shift, below=0):
    upper = (((index + reach + base * below) * mul) >> shift) - below
    return upper, index - base * upper

def lattice_kernel(counts, base, x_ref, grid, e01_a, e01_b, e2_a, e2_b, rhs_a, rhs_b, acc):
    acc[...] = jnp.zeros_like(acc)
    pieces, _, rows, _ = x_ref.shape
    piece = rows * 128
    per_piece = piece // CHUNK
    chunks = pieces * per_piece
    end = [counts[0, 0], counts[0, 0] + counts[0, 1]]
    below = []
    for e in end:
        total = 0
        for p in range(pieces):
            total = total + jnp.clip(e - (base[0] + 2 * p) * piece, 0, piece)
        below.append(total)
    cut0, cut1 = below
    turn0 = (cut0 + CHUNK - 1) // CHUNK
    turn1 = turn0 + (cut1 + CHUNK - 1) // CHUNK - cut0 // CHUNK

    lane = lax.broadcasted_iota(jnp.int32, (1, CHUNK), 1)
    line = lax.broadcasted_iota(jnp.int32, (LINES, CHUNK), 0)
    q0, q1 = [(5 * q).astype(f32) for q in balanced(line, 13, 6, 79, 10)]
    q2 = (5 * lax.broadcasted_iota(jnp.int32, (8, CHUNK), 0)).astype(f32)
    r0, rest = balanced(lax.broadcasted_iota(jnp.int32, (64, CHUNK), 0), 25, 12, 41, 10)
    r1, r2 = balanced(rest, 5, 2, 205, 10, 3)
    r0, r1, r2 = r0.astype(f32), r1.astype(f32), r2.astype(f32)

    def visit(v):
        kind = (v >= turn0).astype(jnp.int32) + (v >= turn1).astype(jnp.int32)
        chunk = jnp.where(kind == 0, v, jnp.where(kind == 1, v - turn0 + cut0 // CHUNK, v - turn1 + cut1 // CHUNK))
        first = jnp.where(kind == 0, 0, jnp.where(kind == 1, cut0, cut1))
        last = jnp.where(kind == 0, cut0, jnp.where(kind == 1, cut1, chunks * CHUNK))
        return kind, chunk, first, last

    def prepare(v, e01, e2, rhs):
        _, chunk, first, last = visit(v)
        here = jnp.minimum(chunk, chunks - 1)
        xs = []
        for d in range(3):
            at = lax.rem(here, per_piece) * (CHUNK // 128)
            parts = [x_ref[here // per_piece, d, pl.ds(at + n, 1)] for n in range(CHUNK // 128)]
            whole = jnp.concatenate(parts, axis=1)
            xs.append(whole - jnp.round(whole))
        c, s = waves(q0 * xs[0] + q1 * xs[1])
        e01[0:LINES] = c
        e01[LINES:] = s
        c, s = waves(q2 * xs[2])
        e2[0:8] = c
        e2[8:16] = s
        where = chunk * CHUNK + lane
        mask = jnp.logical_and(where >= first, where < last).astype(f32)
        c, s = waves(r0 * xs[0] + r1 * xs[1] + r2 * xs[2])
        hi, lo = split(jnp.concatenate([c * mask, s * mask], axis=0))
        rhs[0:128] = hi
        rhs[128:256] = lo

    def gather(v, e01, e2, rhs):
        kind = visit(v)[0]
        weights = rhs[...]
        for l in range(COARSE):
            row = l if l < 7 else l + 2
            hi, lo = split(e01[...] * e2[row:row + 1])
            lhs = jnp.concatenate([hi, lo], axis=0)
            p = lax.dot_general(lhs, weights, (((1,), (1,)), ((), ())), preferred_element_type=f32)
            p = p[0:2 * LINES] + p[2 * LINES:]
            acc[kind, l] += p[:, :128] + p[:, 128:]

    buffers = ((e01_a, e2_a, rhs_a), (e01_b, e2_b, rhs_b))
    prepare(0, *buffers[0])

    def pair(i, _):
        prepare(2 * i + 1, *buffers[1])
        gather(2 * i, *buffers[0])
        prepare(2 * i + 2, *buffers[0])
        gather(2 * i + 1, *buffers[1])
        return 0

    lax.fori_loop(0, (chunks + 2) // 2, pair, 0)

    front = lax.broadcasted_iota(jnp.int32, (LINES, 128), 1) < 64

    def put(q2, sp, a, b):
        plus = b + pltpu.roll(a, 64, axis=1)
        minus = a - pltpu.roll(b, 64, axis=1)
        at = (q2 + 6) * LINES * 8 + sp
        grid[pl.ds(at, LINES, stride=8), :] = jnp.where(front, minus, plus)
        grid[pl.ds(at + 4, LINES, stride=8), :] = jnp.where(front, plus, -minus)

    for sp in range(3):
        put(0, sp, acc[sp, 0, 0:LINES], acc[sp, 0, LINES:])
        for l in range(1, 7):
            cc, sc = acc[sp, l, 0:LINES], acc[sp, l, LINES:]
            cs, ss = acc[sp, l + 6, 0:LINES], acc[sp, l + 6, LINES:]
            put(l, sp, cc - ss, sc + cs)
            put(-l, sp, cc + ss, sc - cs)


def call_lattice(counts, base, x):
    smem = pl.BlockSpec(memory_space=pltpu.SMEM)
    vmem = pl.BlockSpec(memory_space=pltpu.VMEM)
    return pl.pallas_call(
        lattice_kernel,
        out_shape=jax.ShapeDtypeStruct((13 * LINES * 8, 128), f32),
        in_specs=[smem, smem, vmem],
        out_specs=vmem,
        scratch_shapes=[pltpu.VMEM((2 * LINES, CHUNK), f32)] * 2
        + [pltpu.VMEM((16, CHUNK), f32)] * 2
        + [pltpu.VMEM((256, CHUNK), bf16)] * 2
        + [pltpu.VMEM((3, COARSE, 2 * LINES, 128), f32)],
        compiler_params=pltpu.CompilerParams(vmem_limit_bytes=24 * 1024 * 1024),
    )(counts, base, x)


def picks(k_index):
    n = [k_index[d:d + 1] for d in range(3)]
    q, r = zip(*[balanced(v, 5, 2, 205, 10, 6) for v in n])
    jc = 13 * q[0] + q[1]
    sq = jnp.where(jc < 0, 1, 0)
    tile = (jnp.where(jc < 0, -q[2], q[2]) + 6) * LINES + jnp.abs(jc)
    rc = 25 * r[0] + 5 * r[1] + r[2]
    sr = jnp.where(rc < 0, 1, 0)
    lane = lax.broadcasted_iota(jnp.int32, rc.shape, 1)
    shift = (lane - jnp.abs(rc) - 64 * (sr ^ sq)) & 127
    return tile * 256 + sq * 128 + shift


def spread_kernel(plan, k_ref, pos_ref, x_ref, word_ref, slots, stage, word, send_sem, recv_sem, own_sem):
    me = lax.axis_index("ka")
    count = lax.axis_size("ka")
    rows = slots.shape[2]
    barrier = pltpu.get_barrier_semaphore()

    def greet(i, _):
        pl.semaphore_signal(barrier, inc=1, device_id={"ka": lax.rem(me + i, count)}, device_id_type=MESH)
        return 0

    lax.fori_loop(1, count, greet, 0)
    word[...] = picks(k_ref[...])
    pl.semaphore_wait(barrier, count - 1)

    def send(i, _):
        to = lax.rem(me + i, count)
        pltpu.make_async_remote_copy(
            src_ref=pos_ref.at[:, pl.ds(to * rows, rows)],
            dst_ref=slots.at[me],
            send_sem=send_sem.at[0],
            recv_sem=recv_sem.at[0],
            device_id={"ka": to},
            device_id_type=MESH,
        ).start()
        return 0

    lax.fori_loop(1, count, send, 0)
    keep = pltpu.make_async_copy(pos_ref.at[:, pl.ds(me * rows, rows)], slots.at[me], own_sem)
    keep.start()

    def send_word(i, _):
        pltpu.make_async_remote_copy(
            src_ref=word,
            dst_ref=word_ref.at[me],
            send_sem=send_sem.at[1],
            recv_sem=recv_sem.at[1],
            device_id={"ka": lax.rem(me + i, count)},
            device_id_type=MESH,
        ).start()
        return 0

    lax.fori_loop(1, count, send_word, 0)
    word_ref[me] = word[...]
    keep.wait()
    most = slots.at[pl.ds(0, count - 1)]
    pltpu.make_async_copy(most, most, recv_sem.at[0]).wait()
    frame = lax.rem(me // 2, FRAMES)
    base = me - 2 * frame
    for f in range(FRAMES):
        stage[f] = slots[plan[f]]

    def hand_on(i, _):
        to = lax.rem(frame + i, FRAMES)
        pltpu.make_async_remote_copy(
            src_ref=stage.at[to],
            dst_ref=x_ref.at[frame],
            send_sem=send_sem.at[2],
            recv_sem=recv_sem.at[2],
            device_id={"ka": base + 2 * to},
            device_id_type=MESH,
        ).start()
        return 0

    lax.fori_loop(1, FRAMES, hand_on, 0)
    x_ref[frame] = stage[frame]
    words = word_ref.at[pl.ds(0, count - 1)]
    pltpu.make_async_copy(words, words, recv_sem.at[1]).wait()
    rest = x_ref.at[pl.ds(0, FRAMES - 1)]
    pltpu.make_async_copy(rest, rest, recv_sem.at[2]).wait()
    pltpu.make_async_copy(most, most, send_sem.at[0]).wait()
    pltpu.make_async_copy(words, words, send_sem.at[1]).wait()
    pltpu.make_async_copy(rest, rest, send_sem.at[2]).wait()


def call_spread(plan, k_index, positions):
    smem = pl.BlockSpec(memory_space=pltpu.SMEM)
    vmem = pl.BlockSpec(memory_space=pltpu.VMEM)
    count = lax.axis_size("ka")
    rows = positions.shape[2] // (128 * count)
    positions = positions.reshape(3, rows * count, 128)
    return pl.pallas_call(
        spread_kernel,
        out_shape=(
            jax.ShapeDtypeStruct((FRAMES, 3, rows, 128), f32),
            jax.ShapeDtypeStruct((count, 1, k_index.shape[1]), jnp.int32),
        ),
        in_specs=[smem, vmem, pl.BlockSpec(memory_space=pl.ANY)],
        out_specs=(vmem, vmem),
        scratch_shapes=[
            pltpu.VMEM((count, 3, rows, 128), f32),
            pltpu.VMEM((FRAMES, 3, rows, 128), f32),
            pltpu.VMEM((1, k_index.shape[1]), jnp.int32),
            pltpu.SemaphoreType.DMA((3,)),
            pltpu.SemaphoreType.DMA((3,)),
            pltpu.SemaphoreType.DMA,
        ],
        compiler_params=pltpu.CompilerParams(collective_id=0, has_side_effects=True),
    )(plan, k_index, positions)


def pick_blocks(grid, pick, word_ref, modes, blocks):
    lanes = lax.broadcasted_iota(jnp.int32, (8, 128), 1)
    upper = lax.broadcasted_iota(jnp.int32, (8, 128), 0) < 4
    for b in blocks:
        found = jnp.zeros((8, 128), f32)
        for j in range(128):
            word = pick[b, 0, j]
            found = jnp.where(lanes == j, pltpu.roll(grid[word >> 8], word & 127, axis=1), found)
        sign = jnp.where((word_ref[b] & 128) > 0, -1.0, 1.0)
        modes[b] = found * jnp.where(upper, 1.0, sign)


def factors_kernel(scale, grid, word_ref, out_ref, modes, parts, pick, send_sem, recv_sem, own_sem):
    me = lax.axis_index("ka")
    half = lax.axis_index("atoms")
    count = lax.axis_size("ka")
    barrier = pltpu.get_barrier_semaphore()
    fetch = pltpu.make_async_copy(word_ref, pick, own_sem)
    fetch.start()

    def greet(i, _):
        to = lax.rem(me + i, count)
        pl.semaphore_signal(barrier, inc=1, device_id={"ka": to, "atoms": 1 - half}, device_id_type=MESH)

        @pl.when(i < count)
        def _():
            pl.semaphore_signal(barrier, inc=1, device_id={"ka": to, "atoms": half}, device_id_type=MESH)
        return 0

    lax.fori_loop(1, count + 1, greet, 0)
    fetch.wait()
    slot = half * count + me

    def send(i):
        to = lax.rem(me + i + 1, count)

        def copy(h):
            return pltpu.make_async_remote_copy(
                src_ref=modes.at[to],
                dst_ref=parts.at[slot],
                send_sem=send_sem,
                recv_sem=recv_sem,
                device_id={"ka": to, "atoms": h},
                device_id_type=MESH,
            )

        copy(1 - half).start()

        @pl.when(i < count - 1)
        def _():
            copy(half).start()

    def group(g, _):
        pick_blocks(grid, pick, word_ref, modes, [lax.rem(me + GROUP * g + u + 1, count) for u in range(GROUP)])

        @pl.when(g == 1)
        def _():
            pl.semaphore_wait(barrier, 2 * count - 1)
            for u in range(GROUP):
                send(u)

        @pl.when(g > 0)
        def _():
            for u in range(GROUP):
                send(GROUP * g + u)
        return 0

    lax.fori_loop(0, count // GROUP, group, 0)
    parts[slot] = modes[me]
    most = parts.at[pl.ds(0, 2 * count - 1)]
    pltpu.make_async_copy(most, most, recv_sem).wait()
    window = []
    for f in range(FRAMES):
        total = None
        for high in range(2 * count // 16):
            for core in range(2):
                part = parts[high * 16 + f * 2 + core]
                total = part if total is None else total + part
        window.append(total)
    upper = lax.broadcasted_iota(jnp.int32, (8, 128), 0) < 4
    crossed = [jnp.where(upper, 1.0, -1.0) * pltpu.roll(w, 4, axis=0) for w in window]
    pairs = ((0, 0), (0, 1), (0, 2), (1, 1), (1, 2), (2, 2))
    for f in range(FRAMES):
        wave = window[0]
        for t in range(1, FRAMES):
            turn = 2 * math.pi * (f * t % FRAMES) / FRAMES
            wave = wave + math.cos(turn) * window[t] + math.sin(turn) * crossed[t]
        for p, (a, b) in enumerate(pairs):
            value = wave[a:a + 1] * wave[b:b + 1] + wave[4 + a:5 + a] * wave[4 + b:5 + b]
            out_ref[f, p:p + 1] = value * scale
    pltpu.make_async_copy(most, most, send_sem).wait()


def call_factors(grid, words, total_atoms):
    vmem = pl.BlockSpec(memory_space=pltpu.VMEM)
    count = lax.axis_size("ka")
    lanes = words.shape[2]
    return pl.pallas_call(
        functools.partial(factors_kernel, 1.0 / (FRAMES * total_atoms)),
        out_shape=jax.ShapeDtypeStruct((FRAMES, 6, lanes), f32),
        in_specs=[vmem, vmem],
        out_specs=vmem,
        scratch_shapes=[
            pltpu.VMEM((count, 8, lanes), f32),
            pltpu.VMEM((2 * count, 8, lanes), f32),
            pltpu.SMEM(words.shape, jnp.int32),
            pltpu.SemaphoreType.DMA,
            pltpu.SemaphoreType.DMA,
            pltpu.SemaphoreType.DMA,
        ],
        compiler_params=pltpu.CompilerParams(collective_id=1, has_side_effects=True, vmem_limit_bytes=20 * 1024 * 1024),
    )(grid.reshape(13 * LINES, 8, 128), words)


def local(positions, counts, plan, k_index):
    me = lax.axis_index("ka")
    x, words = call_spread(plan, k_index, positions)
    first = me - lax.rem(me // 2, FRAMES) * 2
    grid = call_lattice(counts, first.astype(jnp.int32).reshape(1), x)
    return call_factors(grid, words, positions.shape[2] * lax.axis_size("atoms"))


def solution(mesh):
    return jax.shard_map(
        local,
        mesh=mesh,
        in_specs=(P("ka", None, "atoms"), P("atoms", None), P(), P(None, "ka")),
        out_specs=P(None, None, "ka"),
        check_vma=False,
    )
```

```python
import functools
import math

import jax
import jax.numpy as jnp
import numpy as np
from jax import lax
from jax.experimental import pallas as pl
from jax.experimental.pallas import tpu as pltpu
from jax.sharding import PartitionSpec as P

MESH = pl.DeviceIdType.MESH
FRAMES = 8
LINES = 88
COARSE = 13
CHUNK = 256
GROUP = 4
HOPS = (0, 1, 2, 1)
ORDER = sorted(
    [(z, y, x, c) for c in range(2) for x in range(4) for y in range(4) for z in range(2) if z + y + x + c],
    key=lambda d: -(d[0] + HOPS[d[1]] + HOPS[d[2]]),
)
f32 = jnp.float32
bf16 = jnp.bfloat16

def fit_coefs():
    t = np.cos(np.pi * (np.arange(4000) + 0.5) / 4000) * 0.5
    u = t * t
    a = np.vander(u, 5, increasing=True)
    ps = np.linalg.lstsq(a * t[:, None], np.sin(np.pi * t), rcond=None)[0]
    pc = np.linalg.lstsq(a, np.cos(np.pi * t), rcond=None)[0]
    return [float(x) for x in ps], [float(x) for x in pc]

SIN_C, COS_C = fit_coefs()

def waves(cycles):
    t = cycles - jnp.round(cycles)
    u = t * t
    s = jnp.full_like(u, SIN_C[-1])
    for c in SIN_C[-2::-1]:
        s = s * u + c
    s = s * t
    q = jnp.full_like(u, COS_C[-1])
    for c in COS_C[-2::-1]:
        q = q * u + c
    twice = s + s
    return 1.0 - twice * s, twice * q

def split(x):
    hi = x.astype(bf16)
    lo = (x - hi.astype(f32)).astype(bf16)
    return hi, lo

def balanced(index, base, reach, mul, shift, below=0):
    upper = (((index + reach + base * below) * mul) >> shift) - below
    return upper, index - base * upper

def lattice_kernel(counts_ref, x_ref, grid, e01_a, e01_b, e2_a, e2_b, rhs_a, rhs_b, acc, counts, counts_sem):
    fetch = pltpu.make_async_copy(counts_ref, counts, counts_sem)
    fetch.start()
    me = lax.axis_index("ka")
    base = me - 2 * lax.rem(me // 2, FRAMES)
    acc[...] = jnp.zeros_like(acc)
    fetch.wait()
    pieces, _, rows, _ = x_ref.shape
    piece = rows * 128
    per_piece = piece // CHUNK
    chunks = pieces * per_piece
    end = [counts[0, 0], counts[0, 0] + counts[0, 1]]
    below = []
    for e in end:
        total = 0
        for p in range(pieces):
            total = total + jnp.clip(e - (base + 2 * p) * piece, 0, piece)
        below.append(total)
    cut0, cut1 = below
    turn0 = (cut0 + CHUNK - 1) // CHUNK
    turn1 = turn0 + (cut1 + CHUNK - 1) // CHUNK - cut0 // CHUNK

    lane = lax.broadcasted_iota(jnp.int32, (1, CHUNK), 1)

    def visit(v):
        kind = (v >= turn0).astype(jnp.int32) + (v >= turn1).astype(jnp.int32)
        chunk = jnp.where(kind == 0, v, jnp.where(kind == 1, v - turn0 + cut0 // CHUNK, v - turn1 + cut1 // CHUNK))
        first = jnp.where(kind == 0, 0, jnp.where(kind == 1, cut0, cut1))
        last = jnp.where(kind == 0, cut0, jnp.where(kind == 1, cut1, chunks * CHUNK))
        return kind, chunk, first, last

    def prepare(v, e01, e2, rhs):
        _, chunk, first, last = visit(v)
        here = jnp.minimum(chunk, chunks - 1)
        xs = []
        for d in range(3):
            at = lax.rem(here, per_piece) * (CHUNK // 128)
            parts = [x_ref[here // per_piece, d, pl.ds(at + n, 1)] for n in range(CHUNK // 128)]
            whole = jnp.concatenate(parts, axis=1)
            xs.append(whole - jnp.round(whole))
        where = chunk * CHUNK + lane
        mask = jnp.logical_and(where >= first, where < last).astype(f32)

        def lines(row):
            line = row + lax.broadcasted_iota(jnp.int32, (8, CHUNK), 0)
            q0, q1 = [(5 * q).astype(f32) for q in balanced(line, 13, 6, 79, 10)]
            c, s = waves(q0 * xs[0] + q1 * xs[1])
            e01[row:row + 8] = c
            e01[LINES + row:LINES + row + 8] = s

        def depths():
            q2 = (5 * lax.broadcasted_iota(jnp.int32, (8, CHUNK), 0)).astype(f32)
            c, s = waves(q2 * xs[2])
            e2[0:8] = c
            e2[8:16] = s

        def columns(row):
            index = row + lax.broadcasted_iota(jnp.int32, (16, CHUNK), 0)
            r0, rest = balanced(index, 25, 12, 41, 10)
            r1, r2 = balanced(rest, 5, 2, 205, 10, 3)
            c, s = waves(r0.astype(f32) * xs[0] + r1.astype(f32) * xs[1] + r2.astype(f32) * xs[2])
            for at, value in ((row, c), (64 + row, s)):
                hi, lo = split(value * mask)
                rhs[at:at + 16] = hi
                rhs[128 + at:144 + at] = lo

        steps = [functools.partial(lines, row) for row in range(0, LINES, 8)]
        steps += [functools.partial(columns, row) for row in range(0, 64, 16)]
        return steps + [depths]

    def gather(v, e01, e2, rhs, steps):
        kind = visit(v)[0]
        weights = rhs[...]
        for l in range(0, COARSE, 3):
            some = range(l, min(l + 3, COARSE))
            parts = []
            for m in some:
                row = m if m < 7 else m + 2
                parts += split(e01[...] * e2[row:row + 1])
            lhs = jnp.concatenate(parts, axis=0)
            p = lax.dot_general(lhs, weights, (((1,), (1,)), ((), ())), preferred_element_type=f32)
            for m in some:
                at = (m - l) * 4 * LINES
                one = p[at:at + 2 * LINES] + p[at + 2 * LINES:at + 4 * LINES]
                acc[kind, m] += one[:, :128] + one[:, 128:]
            for step in steps[l * len(steps) // COARSE:min(l + 3, COARSE) * len(steps) // COARSE]:
                step()

    buffers = ((e01_a, e2_a, rhs_a), (e01_b, e2_b, rhs_b))
    for step in prepare(0, *buffers[0]):
        step()

    def pair(i, _):
        gather(2 * i, *buffers[0], prepare(2 * i + 1, *buffers[1]))
        gather(2 * i + 1, *buffers[1], prepare(2 * i + 2, *buffers[0]))
        return 0

    lax.fori_loop(0, (chunks + 2) // 2, pair, 0)

    front = lax.broadcasted_iota(jnp.int32, (LINES, 128), 1) < 64

    def put(q2, sp, a, b):
        plus = b + pltpu.roll(a, 64, axis=1)
        minus = a - pltpu.roll(b, 64, axis=1)
        at = (q2 + 6) * LINES * 8 + sp
        grid[pl.ds(at, LINES, stride=8), :] = jnp.where(front, minus, plus)
        grid[pl.ds(at + 4, LINES, stride=8), :] = jnp.where(front, plus, -minus)

    for sp in range(3):
        put(0, sp, acc[sp, 0, 0:LINES], acc[sp, 0, LINES:])
        for l in range(1, 7):
            cc, sc = acc[sp, l, 0:LINES], acc[sp, l, LINES:]
            cs, ss = acc[sp, l + 6, 0:LINES], acc[sp, l + 6, LINES:]
            put(l, sp, cc - ss, sc + cs)
            put(-l, sp, cc + ss, sc - cs)


def call_lattice(counts, x):
    vmem = pl.BlockSpec(memory_space=pltpu.VMEM)
    return pl.pallas_call(
        lattice_kernel,
        out_shape=jax.ShapeDtypeStruct((13 * LINES * 8, 128), f32),
        in_specs=[vmem, vmem],
        out_specs=vmem,
        scratch_shapes=[pltpu.VMEM((2 * LINES, CHUNK), f32)] * 2
        + [pltpu.VMEM((16, CHUNK), f32)] * 2
        + [pltpu.VMEM((256, CHUNK), bf16)] * 2
        + [pltpu.VMEM((3, COARSE, 2 * LINES, 128), f32), pltpu.SMEM(counts.shape, jnp.int32), pltpu.SemaphoreType.DMA],
        compiler_params=pltpu.CompilerParams(vmem_limit_bytes=24 * 1024 * 1024),
    )(counts, x)


def picks(k_index):
    n = [k_index[d:d + 1] for d in range(3)]
    q, r = zip(*[balanced(v, 5, 2, 205, 10, 6) for v in n])
    jc = 13 * q[0] + q[1]
    sq = jnp.where(jc < 0, 1, 0)
    tile = (jnp.where(jc < 0, -q[2], q[2]) + 6) * LINES + jnp.abs(jc)
    rc = 25 * r[0] + 5 * r[1] + r[2]
    sr = jnp.where(rc < 0, 1, 0)
    lane = lax.broadcasted_iota(jnp.int32, rc.shape, 1)
    shift = (lane - jnp.abs(rc) - 64 * (sr ^ sq)) & 127
    return tile * 256 + sq * 128 + shift


def spread_kernel(small_ref, pos_ref, x_ref, word_ref, bound_ref, slots, stage, plan, send_sem, recv_sem, own_sem):
    me = lax.axis_index("ka")
    count = lax.axis_size("ka")
    frame = lax.rem(me // 2, FRAMES)
    base = me - 2 * frame
    wide = 2 * FRAMES
    groups = count // FRAMES
    mine = me // wide * 2 + lax.rem(me, 2)
    barrier = pltpu.get_barrier_semaphore()
    fetches = [
        pltpu.make_async_copy(small_ref, plan, own_sem.at[0]),
        pltpu.make_async_copy(pos_ref.at[:, me], slots.at[me], own_sem.at[1]),
    ]
    for fetch in fetches:
        fetch.start()

    def greet(i, _):
        pl.semaphore_signal(barrier, inc=1, device_id={"ka": lax.rem(me + i, count)}, device_id_type=MESH)
        return 0

    lax.fori_loop(1, count, greet, 0)
    bound_ref[...] = small_ref[3:4]
    word_ref[mine, pl.ds(frame, 1)] = picks(small_ref[0:3])
    pl.semaphore_wait(barrier, count - 1)

    def share(i, _):
        to = lax.rem(frame + i, FRAMES)
        pltpu.make_async_remote_copy(
            src_ref=word_ref.at[mine, pl.ds(frame, 1)],
            dst_ref=word_ref.at[mine, pl.ds(frame, 1)],
            send_sem=send_sem.at[1],
            recv_sem=recv_sem.at[1],
            device_id={"ka": base + 2 * to},
            device_id_type=MESH,
        ).start()
        return 0

    lax.fori_loop(1, FRAMES, share, 0)

    z, y, x, core = me // 32, lax.rem(me // 8, 4), lax.rem(me // 2, 4), lax.rem(me, 2)
    for dz, dy, dx, dc in ORDER:
        to = lax.rem(z + dz, 2) * 32 + lax.rem(y + dy, 4) * 8 + lax.rem(x + dx, 4) * 2 + lax.rem(core + dc, 2)
        pltpu.make_async_remote_copy(
            src_ref=pos_ref.at[:, to],
            dst_ref=slots.at[me],
            send_sem=send_sem.at[0],
            recv_sem=recv_sem.at[0],
            device_id={"ka": to},
            device_id_type=MESH,
        ).start()
    row = word_ref.at[mine, pl.ds(0, FRAMES - 1)]
    pltpu.make_async_copy(row, row, recv_sem.at[1]).wait()

    def share_group(i, _):
        to = lax.rem(mine + i, groups)
        pltpu.make_async_remote_copy(
            src_ref=word_ref.at[mine],
            dst_ref=word_ref.at[mine],
            send_sem=send_sem.at[3],
            recv_sem=recv_sem.at[3],
            device_id={"ka": to // 2 * wide + 2 * frame + lax.rem(to, 2)},
            device_id_type=MESH,
        ).start()
        return 0

    lax.fori_loop(1, groups, share_group, 0)
    for fetch in fetches:
        fetch.wait()
    most = slots.at[pl.ds(0, count - 1)]
    pltpu.make_async_copy(most, most, recv_sem.at[0]).wait()
    for f in range(FRAMES):
        stage[f] = slots[plan[3, 8 + f]]

    def hand_on(i, _):
        to = lax.rem(frame + i, FRAMES)
        pltpu.make_async_remote_copy(
            src_ref=stage.at[to],
            dst_ref=x_ref.at[frame],
            send_sem=send_sem.at[2],
            recv_sem=recv_sem.at[2],
            device_id={"ka": base + 2 * to},
            device_id_type=MESH,
        ).start()
        return 0

    lax.fori_loop(1, FRAMES, hand_on, 0)
    x_ref[frame] = stage[frame]
    words = word_ref.at[pl.ds(0, groups - 1)]
    rest = x_ref.at[pl.ds(0, FRAMES - 1)]
    pltpu.make_async_copy(words, words, recv_sem.at[3]).wait()
    pltpu.make_async_copy(most, most, send_sem.at[0]).wait()
    pltpu.make_async_copy(row, row, send_sem.at[1]).wait()
    pltpu.make_async_copy(words, words, send_sem.at[3]).wait()
    pltpu.make_async_copy(rest, rest, recv_sem.at[2]).wait()
    pltpu.make_async_copy(rest, rest, send_sem.at[2]).wait()


def call_spread(plan, k_index, counts, positions):
    hbm = pl.BlockSpec(memory_space=pltpu.HBM)
    vmem = pl.BlockSpec(memory_space=pltpu.VMEM)
    count = lax.axis_size("ka")
    rows = positions.shape[2] // (128 * count)
    lanes = k_index.shape[1]
    small = jnp.pad(k_index, ((0, 1), (0, 0))) + jnp.pad(counts, ((3, 0), (0, lanes - 3))) + jnp.pad(plan[None], ((3, 0), (8, lanes - 16)))
    return pl.pallas_call(
        spread_kernel,
        out_shape=(
            jax.ShapeDtypeStruct((FRAMES, 3, rows, 128), f32),
            jax.ShapeDtypeStruct((count // FRAMES, FRAMES, lanes), jnp.int32),
            jax.ShapeDtypeStruct((1, lanes), jnp.int32),
        ),
        in_specs=[vmem, hbm],
        out_specs=(vmem, vmem, vmem),
        scratch_shapes=[
            pltpu.VMEM((count, 3, rows, 128), f32),
            pltpu.VMEM((FRAMES, 3, rows, 128), f32),
            pltpu.SMEM((4, lanes), jnp.int32),
            pltpu.SemaphoreType.DMA((4,)),
            pltpu.SemaphoreType.DMA((4,)),
            pltpu.SemaphoreType.DMA((2,)),
        ],
        compiler_params=pltpu.CompilerParams(collective_id=0, has_side_effects=True, vmem_limit_bytes=8 * 1024 * 1024),
    )(small, positions.reshape(3, count, rows, 128))


def pick_blocks(grid, pick, word_ref, modes, blocks, places):
    lanes = lax.broadcasted_iota(jnp.int32, (8, 128), 1)
    upper = lax.broadcasted_iota(jnp.int32, (8, 128), 0) < 4
    for b, at in zip(blocks, places):
        group, lead = b // (2 * FRAMES) * 2 + lax.rem(b, 2), lax.rem(b // 2, FRAMES)
        found = jnp.zeros((8, 128), f32)
        for j in range(128):
            word = pick[group, lead, j]
            found = jnp.where(lanes == j, pltpu.roll(grid[word >> 8], word & 127, axis=1), found)
        sign = jnp.where((word_ref[group, pl.ds(lead, 1)] & 128) > 0, -1.0, 1.0)
        modes[at] = found * jnp.where(upper, 1.0, sign)


def factors_kernel(scale, grid, word_ref, out_ref, modes, spare, parts, beside, pick, send_sem, recv_sem, own_sem):
    me = lax.axis_index("ka")
    half = lax.axis_index("atoms")
    chips = lax.axis_size("ka") // 2
    chip, core = me // 2, lax.rem(me, 2)
    barrier = pltpu.get_barrier_semaphore()
    fetch = pltpu.make_async_copy(word_ref, pick, own_sem)
    fetch.start()

    def greet(i, _):
        to = 2 * lax.rem(chip + i, chips) + core
        pl.semaphore_signal(barrier, inc=1, device_id={"ka": to, "atoms": 1 - half}, device_id_type=MESH)

        @pl.when(i < chips)
        def _():
            pl.semaphore_signal(barrier, inc=1, device_id={"ka": to, "atoms": half}, device_id_type=MESH)
        return 0

    pl.semaphore_signal(barrier, inc=1, device_id={"ka": 2 * chip + 1 - core}, device_id_type=MESH)
    lax.fori_loop(1, chips + 1, greet, 0)
    fetch.wait()
    slot = half * chips + chip

    def place(i):
        return lax.rem(chip + i + 1, chips)

    def hand_over(g):
        pltpu.make_async_remote_copy(
            src_ref=spare.at[pl.ds(GROUP * g, GROUP)],
            dst_ref=beside.at[pl.ds(GROUP * g, GROUP)],
            send_sem=send_sem.at[0],
            recv_sem=recv_sem.at[0],
            device_id={"ka": 2 * chip + 1 - core},
            device_id_type=MESH,
        ).start()

    def first_half(g, _):
        at = [GROUP * g + u for u in range(GROUP)]
        pick_blocks(grid, pick, word_ref, spare, [2 * place(i) + 1 - core for i in at], at)

        @pl.when(g == 1)
        def _():
            pl.semaphore_wait(barrier, 2 * chips)
            hand_over(0)

        @pl.when(g > 0)
        def _():
            hand_over(g)
        return 0

    lax.fori_loop(0, chips // GROUP, first_half, 0)
    handed = beside.at[pl.ds(0, chips)]

    def send(i):
        to = place(i)
        modes[i] += beside[i]

        def copy(h):
            return pltpu.make_async_remote_copy(
                src_ref=modes.at[i],
                dst_ref=parts.at[slot],
                send_sem=send_sem.at[1],
                recv_sem=recv_sem.at[1],
                device_id={"ka": 2 * to + core, "atoms": h},
                device_id_type=MESH,
            )

        copy(1 - half).start()

        @pl.when(i < chips - 1)
        def _():
            copy(half).start()

    def second_half(g, _):
        at = [GROUP * g + u for u in range(GROUP)]
        pick_blocks(grid, pick, word_ref, modes, [2 * place(i) + core for i in at], at)

        @pl.when(g == 1)
        def _():
            pltpu.make_async_copy(handed, handed, recv_sem.at[0]).wait()
            for u in range(GROUP):
                send(u)

        @pl.when(g > 0)
        def _():
            for i in at:
                send(i)
        return 0

    lax.fori_loop(0, chips // GROUP, second_half, 0)
    parts[slot] = modes[chips - 1]
    most = parts.at[pl.ds(0, 2 * chips - 1)]
    pltpu.make_async_copy(most, most, recv_sem.at[1]).wait()
    window = []
    for f in range(FRAMES):
        total = None
        for high in range(2 * chips // FRAMES):
            part = parts[high * FRAMES + f]
            total = part if total is None else total + part
        window.append(total)
    upper = lax.broadcasted_iota(jnp.int32, (8, 128), 0) < 4
    crossed = [jnp.where(upper, 1.0, -1.0) * pltpu.roll(w, 4, axis=0) for w in window]
    pairs = ((0, 0), (0, 1), (0, 2), (1, 1), (1, 2), (2, 2))
    for f in range(FRAMES):
        wave = window[0]
        for t in range(1, FRAMES):
            turn = 2 * math.pi * (f * t % FRAMES) / FRAMES
            wave = wave + math.cos(turn) * window[t] + math.sin(turn) * crossed[t]
        for p, (a, b) in enumerate(pairs):
            value = wave[a:a + 1] * wave[b:b + 1] + wave[4 + a:5 + a] * wave[4 + b:5 + b]
            out_ref[p, f:f + 1] = value * scale
    pltpu.make_async_copy(handed, handed, send_sem.at[0]).wait()
    pltpu.make_async_copy(most, most, send_sem.at[1]).wait()


def call_factors(grid, words, total_atoms):
    vmem = pl.BlockSpec(memory_space=pltpu.VMEM)
    count = lax.axis_size("ka")
    lanes = words.shape[2]
    return pl.pallas_call(
        functools.partial(factors_kernel, 1.0 / (FRAMES * total_atoms)),
        out_shape=jax.ShapeDtypeStruct((6, FRAMES, lanes), f32),
        in_specs=[vmem, vmem],
        out_specs=vmem,
        scratch_shapes=[
            pltpu.VMEM((count // 2, 8, lanes), f32),
            pltpu.VMEM((count // 2, 8, lanes), f32),
            pltpu.VMEM((count, 8, lanes), f32),
            pltpu.VMEM((count // 2 + 1, 8, lanes), f32),
            pltpu.SMEM(words.shape, jnp.int32),
            pltpu.SemaphoreType.DMA((2,)),
            pltpu.SemaphoreType.DMA((2,)),
            pltpu.SemaphoreType.DMA,
        ],
        compiler_params=pltpu.CompilerParams(collective_id=1, has_side_effects=True, vmem_limit_bytes=20 * 1024 * 1024),
    )(grid.reshape(13 * LINES, 8, 128), words)


def local(positions, counts, plan, k_index):
    x, words, bounds = call_spread(plan, k_index, counts, positions)
    grid = call_lattice(bounds, x)
    factors = call_factors(grid, words, positions.shape[2] * lax.axis_size("atoms"))
    return jnp.transpose(factors, (1, 0, 2))


def solution(mesh):
    return jax.shard_map(
        local,
        mesh=mesh,
        in_specs=(P("ka", None, "atoms"), P("atoms", None), P(), P(None, "ka")),
        out_specs=P(None, None, "ka"),
        check_vma=False,
    )
```

```python
import functools
import math

import jax
import jax.numpy as jnp
import numpy as np
from jax import lax
from jax.experimental import pallas as pl
from jax.experimental.pallas import tpu as pltpu
from jax.sharding import PartitionSpec as P

MESH = pl.DeviceIdType.MESH
FRAMES = 8
LINES = 88
COARSE = 13
CHUNK = 256
GROUP = 4
HOPS = (0, 1, 2, 1)
ORDER = sorted(
    [(z, y, x, c) for c in range(2) for x in range(4) for y in range(4) for z in range(2) if z + y + x + c],
    key=lambda d: -(d[0] + HOPS[d[1]] + HOPS[d[2]]),
)
f32 = jnp.float32
bf16 = jnp.bfloat16

def fit_coefs():
    t = np.cos(np.pi * (np.arange(4000) + 0.5) / 4000) * 0.5
    u = t * t
    a = np.vander(u, 5, increasing=True)
    ps = np.linalg.lstsq(a * t[:, None], np.sin(np.pi * t), rcond=None)[0]
    pc = np.linalg.lstsq(a, np.cos(np.pi * t), rcond=None)[0]
    return [float(x) for x in ps], [float(x) for x in pc]

SIN_C, COS_C = fit_coefs()

def waves(cycles):
    t = cycles - jnp.round(cycles)
    u = t * t
    s = jnp.full_like(u, SIN_C[-1])
    for c in SIN_C[-2::-1]:
        s = s * u + c
    s = s * t
    q = jnp.full_like(u, COS_C[-1])
    for c in COS_C[-2::-1]:
        q = q * u + c
    twice = s + s
    return 1.0 - twice * s, twice * q

def split(x):
    hi = x.astype(bf16)
    lo = (x - hi.astype(f32)).astype(bf16)
    return hi, lo

def balanced(index, base, reach, mul, shift, below=0):
    upper = (((index + reach + base * below) * mul) >> shift) - below
    return upper, index - base * upper

def lattice_kernel(counts_ref, x_ref, grid, e01_a, e01_b, e2_a, e2_b, rhs_a, rhs_b, acc, counts, counts_sem):
    fetch = pltpu.make_async_copy(counts_ref, counts, counts_sem)
    fetch.start()
    me = lax.axis_index("ka")
    base = me - 2 * lax.rem(me // 2, FRAMES)
    acc[...] = jnp.zeros_like(acc)
    fetch.wait()
    pieces, _, rows, _ = x_ref.shape
    piece = rows * 128
    per_piece = piece // CHUNK
    chunks = pieces * per_piece
    end = [counts[0, 0], counts[0, 0] + counts[0, 1]]
    below = []
    for e in end:
        total = 0
        for p in range(pieces):
            total = total + jnp.clip(e - (base + 2 * p) * piece, 0, piece)
        below.append(total)
    cut0, cut1 = below
    turn0 = (cut0 + CHUNK - 1) // CHUNK
    turn1 = turn0 + (cut1 + CHUNK - 1) // CHUNK - cut0 // CHUNK
    visits = turn1 + chunks - cut1 // CHUNK

    lane = lax.broadcasted_iota(jnp.int32, (1, CHUNK), 1)

    def visit(v):
        kind = (v >= turn0).astype(jnp.int32) + (v >= turn1).astype(jnp.int32)
        chunk = jnp.where(kind == 0, v, jnp.where(kind == 1, v - turn0 + cut0 // CHUNK, v - turn1 + cut1 // CHUNK))
        first = jnp.where(kind == 0, 0, jnp.where(kind == 1, cut0, cut1))
        last = jnp.where(kind == 0, cut0, jnp.where(kind == 1, cut1, chunks * CHUNK))
        return kind, chunk, first, last

    def prepare(v, e01, e2, rhs):
        _, chunk, first, last = visit(v)
        here = jnp.minimum(chunk, chunks - 1)
        xs = []
        for d in range(3):
            at = lax.rem(here, per_piece) * (CHUNK // 128)
            parts = [x_ref[here // per_piece, d, pl.ds(at + n, 1)] for n in range(CHUNK // 128)]
            whole = jnp.concatenate(parts, axis=1)
            xs.append(whole - jnp.round(whole))
        where = chunk * CHUNK + lane
        mask = jnp.logical_and(where >= first, where < last).astype(f32)

        def lines(row):
            line = row + lax.broadcasted_iota(jnp.int32, (8, CHUNK), 0)
            q0, q1 = [(5 * q).astype(f32) for q in balanced(line, 13, 6, 79, 10)]
            c, s = waves(q0 * xs[0] + q1 * xs[1])
            e01[row:row + 8] = c
            e01[LINES + row:LINES + row + 8] = s

        def depths():
            q2 = (5 * lax.broadcasted_iota(jnp.int32, (8, CHUNK), 0)).astype(f32)
            c, s = waves(q2 * xs[2])
            e2[0:8] = c
            e2[8:16] = s

        def columns(row):
            index = row + lax.broadcasted_iota(jnp.int32, (16, CHUNK), 0)
            r0, rest = balanced(index, 25, 12, 41, 10)
            r1, r2 = balanced(rest, 5, 2, 205, 10, 3)
            c, s = waves(r0.astype(f32) * xs[0] + r1.astype(f32) * xs[1] + r2.astype(f32) * xs[2])
            for at, value in ((row, c), (64 + row, s)):
                hi, lo = split(value * mask)
                rhs[at:at + 16] = hi
                rhs[128 + at:144 + at] = lo

        steps = [functools.partial(lines, row) for row in range(0, LINES, 8)]
        steps += [functools.partial(columns, row) for row in range(0, 64, 16)]
        return steps + [depths]

    def gather(v, e01, e2, rhs, steps):
        kind = visit(v)[0]
        weights = rhs[...]
        for l in range(0, COARSE, 3):
            some = range(l, min(l + 3, COARSE))
            parts = []
            for m in some:
                row = m if m < 7 else m + 2
                parts += split(e01[...] * e2[row:row + 1])
            lhs = jnp.concatenate(parts, axis=0)
            p = lax.dot_general(lhs, weights, (((1,), (1,)), ((), ())), preferred_element_type=f32)
            for m in some:
                at = (m - l) * 4 * LINES
                one = p[at:at + 2 * LINES] + p[at + 2 * LINES:at + 4 * LINES]
                acc[kind, m] += one[:, :128] + one[:, 128:]
            for step in steps[l * len(steps) // COARSE:min(l + 3, COARSE) * len(steps) // COARSE]:
                step()

    buffers = ((e01_a, e2_a, rhs_a), (e01_b, e2_b, rhs_b))
    for step in prepare(0, *buffers[0]):
        step()

    def pair(i, _):
        gather(2 * i, *buffers[0], prepare(2 * i + 1, *buffers[1]))
        gather(2 * i + 1, *buffers[1], prepare(2 * i + 2, *buffers[0]))
        return 0

    lax.fori_loop(0, chunks // 2, pair, 0)

    @pl.when(visits > chunks)
    def _():
        gather(chunks, *buffers[0], [])

    @pl.when(visits > chunks + 1)
    def _():
        for step in prepare(chunks + 1, *buffers[1]):
            step()
        gather(chunks + 1, *buffers[1], [])

    front = lax.broadcasted_iota(jnp.int32, (LINES, 128), 1) < 64

    def put(q2, sp, a, b):
        plus = b + pltpu.roll(a, 64, axis=1)
        minus = a - pltpu.roll(b, 64, axis=1)
        at = (q2 + 6) * LINES * 8 + sp
        grid[pl.ds(at, LINES, stride=8), :] = jnp.where(front, minus, plus)
        grid[pl.ds(at + 4, LINES, stride=8), :] = jnp.where(front, plus, -minus)

    for sp in range(3):
        put(0, sp, acc[sp, 0, 0:LINES], acc[sp, 0, LINES:])
        for l in range(1, 7):
            cc, sc = acc[sp, l, 0:LINES], acc[sp, l, LINES:]
            cs, ss = acc[sp, l + 6, 0:LINES], acc[sp, l + 6, LINES:]
            put(l, sp, cc - ss, sc + cs)
            put(-l, sp, cc + ss, sc - cs)


def call_lattice(counts, x):
    vmem = pl.BlockSpec(memory_space=pltpu.VMEM)
    return pl.pallas_call(
        lattice_kernel,
        out_shape=jax.ShapeDtypeStruct((13 * LINES * 8, 128), f32),
        in_specs=[vmem, vmem],
        out_specs=vmem,
        scratch_shapes=[pltpu.VMEM((2 * LINES, CHUNK), f32)] * 2
        + [pltpu.VMEM((16, CHUNK), f32)] * 2
        + [pltpu.VMEM((256, CHUNK), bf16)] * 2
        + [pltpu.VMEM((3, COARSE, 2 * LINES, 128), f32), pltpu.SMEM(counts.shape, jnp.int32), pltpu.SemaphoreType.DMA],
        compiler_params=pltpu.CompilerParams(vmem_limit_bytes=24 * 1024 * 1024),
    )(counts, x)


def picks(k_index):
    n = [k_index[d:d + 1] for d in range(3)]
    q, r = zip(*[balanced(v, 5, 2, 205, 10, 6) for v in n])
    jc = 13 * q[0] + q[1]
    sq = jnp.where(jc < 0, 1, 0)
    tile = (jnp.where(jc < 0, -q[2], q[2]) + 6) * LINES + jnp.abs(jc)
    rc = 25 * r[0] + 5 * r[1] + r[2]
    sr = jnp.where(rc < 0, 1, 0)
    lane = lax.broadcasted_iota(jnp.int32, rc.shape, 1)
    shift = (lane - jnp.abs(rc) - 64 * (sr ^ sq)) & 127
    return tile * 256 + sq * 128 + shift


def spread_kernel(small_ref, pos_ref, x_ref, word_ref, bound_ref, slots, stage, plan, send_sem, recv_sem, own_sem):
    me = lax.axis_index("ka")
    count = lax.axis_size("ka")
    frame = lax.rem(me // 2, FRAMES)
    base = me - 2 * frame
    wide = 2 * FRAMES
    groups = count // FRAMES
    mine = me // wide * 2 + lax.rem(me, 2)
    barrier = pltpu.get_barrier_semaphore()
    fetches = [
        pltpu.make_async_copy(small_ref, plan, own_sem.at[0]),
        pltpu.make_async_copy(pos_ref.at[:, me], slots.at[me], own_sem.at[1]),
    ]
    for fetch in fetches:
        fetch.start()

    def greet(i, _):
        pl.semaphore_signal(barrier, inc=1, device_id={"ka": lax.rem(me + i, count)}, device_id_type=MESH)
        return 0

    lax.fori_loop(1, count, greet, 0)
    bound_ref[...] = small_ref[3:4]
    word_ref[mine, pl.ds(frame, 1)] = picks(small_ref[0:3])
    pl.semaphore_wait(barrier, count - 1)

    def share(i, _):
        to = lax.rem(frame + i, FRAMES)
        pltpu.make_async_remote_copy(
            src_ref=word_ref.at[mine, pl.ds(frame, 1)],
            dst_ref=word_ref.at[mine, pl.ds(frame, 1)],
            send_sem=send_sem.at[1],
            recv_sem=recv_sem.at[1],
            device_id={"ka": base + 2 * to},
            device_id_type=MESH,
        ).start()
        return 0

    lax.fori_loop(1, FRAMES, share, 0)

    z, y, x, core = me // 32, lax.rem(me // 8, 4), lax.rem(me // 2, 4), lax.rem(me, 2)
    for dz, dy, dx, dc in ORDER:
        to = lax.rem(z + dz, 2) * 32 + lax.rem(y + dy, 4) * 8 + lax.rem(x + dx, 4) * 2 + lax.rem(core + dc, 2)
        pltpu.make_async_remote_copy(
            src_ref=pos_ref.at[:, to],
            dst_ref=slots.at[me],
            send_sem=send_sem.at[0],
            recv_sem=recv_sem.at[0],
            device_id={"ka": to},
            device_id_type=MESH,
        ).start()
    row = word_ref.at[mine, pl.ds(0, FRAMES - 1)]
    pltpu.make_async_copy(row, row, recv_sem.at[1]).wait()

    def share_group(i, _):
        to = lax.rem(mine + i, groups)
        pltpu.make_async_remote_copy(
            src_ref=word_ref.at[mine],
            dst_ref=word_ref.at[mine],
            send_sem=send_sem.at[3],
            recv_sem=recv_sem.at[3],
            device_id={"ka": to // 2 * wide + 2 * frame + lax.rem(to, 2)},
            device_id_type=MESH,
        ).start()
        return 0

    lax.fori_loop(1, groups, share_group, 0)
    for fetch in fetches:
        fetch.wait()
    most = slots.at[pl.ds(0, count - 1)]
    pltpu.make_async_copy(most, most, recv_sem.at[0]).wait()
    for f in range(FRAMES):
        stage[f] = slots[plan[3, 8 + f]]

    def hand_on(i, _):
        to = lax.rem(frame + i, FRAMES)
        pltpu.make_async_remote_copy(
            src_ref=stage.at[to],
            dst_ref=x_ref.at[frame],
            send_sem=send_sem.at[2],
            recv_sem=recv_sem.at[2],
            device_id={"ka": base + 2 * to},
            device_id_type=MESH,
        ).start()
        return 0

    lax.fori_loop(1, FRAMES, hand_on, 0)
    x_ref[frame] = stage[frame]
    words = word_ref.at[pl.ds(0, groups - 1)]
    rest = x_ref.at[pl.ds(0, FRAMES - 1)]
    pltpu.make_async_copy(words, words, recv_sem.at[3]).wait()
    pltpu.make_async_copy(most, most, send_sem.at[0]).wait()
    pltpu.make_async_copy(row, row, send_sem.at[1]).wait()
    pltpu.make_async_copy(words, words, send_sem.at[3]).wait()
    pltpu.make_async_copy(rest, rest, recv_sem.at[2]).wait()
    pltpu.make_async_copy(rest, rest, send_sem.at[2]).wait()


def call_spread(plan, k_index, counts, positions):
    hbm = pl.BlockSpec(memory_space=pltpu.HBM)
    vmem = pl.BlockSpec(memory_space=pltpu.VMEM)
    count = lax.axis_size("ka")
    rows = positions.shape[2] // (128 * count)
    lanes = k_index.shape[1]
    small = jnp.pad(k_index, ((0, 1), (0, 0))) + jnp.pad(counts, ((3, 0), (0, lanes - 3))) + jnp.pad(plan[None], ((3, 0), (8, lanes - 16)))
    return pl.pallas_call(
        spread_kernel,
        out_shape=(
            jax.ShapeDtypeStruct((FRAMES, 3, rows, 128), f32),
            jax.ShapeDtypeStruct((count // FRAMES, FRAMES, lanes), jnp.int32),
            jax.ShapeDtypeStruct((1, lanes), jnp.int32),
        ),
        in_specs=[vmem, hbm],
        out_specs=(vmem, vmem, vmem),
        scratch_shapes=[
            pltpu.VMEM((count, 3, rows, 128), f32),
            pltpu.VMEM((FRAMES, 3, rows, 128), f32),
            pltpu.SMEM((4, lanes), jnp.int32),
            pltpu.SemaphoreType.DMA((4,)),
            pltpu.SemaphoreType.DMA((4,)),
            pltpu.SemaphoreType.DMA((2,)),
        ],
        compiler_params=pltpu.CompilerParams(collective_id=0, has_side_effects=True, vmem_limit_bytes=55000 * 1024),
    )(small, positions.reshape(3, count, rows, 128))


def pick_blocks(grid, pick, word_ref, modes, blocks, places):
    lanes = lax.broadcasted_iota(jnp.int32, (8, 128), 1)
    upper = lax.broadcasted_iota(jnp.int32, (8, 128), 0) < 4
    for b, at in zip(blocks, places):
        group, lead = b // (2 * FRAMES) * 2 + lax.rem(b, 2), lax.rem(b // 2, FRAMES)
        found = jnp.zeros((8, 128), f32)
        for j in range(128):
            word = pick[group, lead, j]
            found = jnp.where(lanes == j, pltpu.roll(grid[word >> 8], word & 127, axis=1), found)
        sign = jnp.where((word_ref[group, pl.ds(lead, 1)] & 128) > 0, -1.0, 1.0)
        modes[at] = found * jnp.where(upper, 1.0, sign)


def factors_kernel(scale, grid, word_ref, out_ref, modes, spare, parts, beside, pick, send_sem, recv_sem, own_sem):
    me = lax.axis_index("ka")
    half = lax.axis_index("atoms")
    chips = lax.axis_size("ka") // 2
    chip, core = me // 2, lax.rem(me, 2)
    barrier = pltpu.get_barrier_semaphore()
    fetch = pltpu.make_async_copy(word_ref, pick, own_sem)
    fetch.start()

    def greet(i, _):
        to = 2 * lax.rem(chip + i, chips) + core
        pl.semaphore_signal(barrier, inc=1, device_id={"ka": to, "atoms": 1 - half}, device_id_type=MESH)

        @pl.when(i < chips)
        def _():
            pl.semaphore_signal(barrier, inc=1, device_id={"ka": to, "atoms": half}, device_id_type=MESH)
        return 0

    pl.semaphore_signal(barrier, inc=1, device_id={"ka": 2 * chip + 1 - core}, device_id_type=MESH)
    lax.fori_loop(1, chips + 1, greet, 0)
    fetch.wait()
    slot = half * chips + chip

    def place(i):
        return lax.rem(chip + i + 1, chips)

    def hand_over(g):
        pltpu.make_async_remote_copy(
            src_ref=spare.at[pl.ds(GROUP * g, GROUP)],
            dst_ref=beside.at[pl.ds(GROUP * g, GROUP)],
            send_sem=send_sem.at[0],
            recv_sem=recv_sem.at[0],
            device_id={"ka": 2 * chip + 1 - core},
            device_id_type=MESH,
        ).start()

    def first_half(g, _):
        at = [GROUP * g + u for u in range(GROUP)]
        pick_blocks(grid, pick, word_ref, spare, [2 * place(i) + 1 - core for i in at], at)

        @pl.when(g == 1)
        def _():
            pl.semaphore_wait(barrier, 2 * chips)
            hand_over(0)

        @pl.when(g > 0)
        def _():
            hand_over(g)
        return 0

    lax.fori_loop(0, chips // GROUP, first_half, 0)
    handed = beside.at[pl.ds(0, chips)]

    def send(i):
        to = place(i)
        modes[i] += beside[i]

        def copy(h):
            return pltpu.make_async_remote_copy(
                src_ref=modes.at[i],
                dst_ref=parts.at[slot],
                send_sem=send_sem.at[1],
                recv_sem=recv_sem.at[1],
                device_id={"ka": 2 * to + core, "atoms": h},
                device_id_type=MESH,
            )

        copy(1 - half).start()

        @pl.when(i < chips - 1)
        def _():
            copy(half).start()

    def second_half(g, _):
        at = [GROUP * g + u for u in range(GROUP)]
        pick_blocks(grid, pick, word_ref, modes, [2 * place(i) + core for i in at], at)

        @pl.when(g == 1)
        def _():
            pltpu.make_async_copy(handed, handed, recv_sem.at[0]).wait()
            for u in range(GROUP):
                send(u)

        @pl.when(g > 0)
        def _():
            for i in at:
                send(i)
        return 0

    lax.fori_loop(0, chips // GROUP, second_half, 0)
    parts[slot] = modes[chips - 1]
    most = parts.at[pl.ds(0, 2 * chips - 1)]
    pltpu.make_async_copy(most, most, recv_sem.at[1]).wait()
    window = []
    for f in range(FRAMES):
        total = None
        for high in range(2 * chips // FRAMES):
            part = parts[high * FRAMES + f]
            total = part if total is None else total + part
        window.append(total)
    upper = lax.broadcasted_iota(jnp.int32, (8, 128), 0) < 4
    crossed = [jnp.where(upper, 1.0, -1.0) * pltpu.roll(w, 4, axis=0) for w in window]
    pairs = ((0, 0), (0, 1), (0, 2), (1, 1), (1, 2), (2, 2))
    for f in range(FRAMES):
        wave = window[0]
        for t in range(1, FRAMES):
            turn = 2 * math.pi * (f * t % FRAMES) / FRAMES
            wave = wave + math.cos(turn) * window[t] + math.sin(turn) * crossed[t]
        for p, (a, b) in enumerate(pairs):
            value = wave[a:a + 1] * wave[b:b + 1] + wave[4 + a:5 + a] * wave[4 + b:5 + b]
            out_ref[p, f:f + 1] = value * scale
    pltpu.make_async_copy(handed, handed, send_sem.at[0]).wait()
    pltpu.make_async_copy(most, most, send_sem.at[1]).wait()


def call_factors(grid, words, total_atoms):
    vmem = pl.BlockSpec(memory_space=pltpu.VMEM)
    count = lax.axis_size("ka")
    lanes = words.shape[2]
    return pl.pallas_call(
        functools.partial(factors_kernel, 1.0 / (FRAMES * total_atoms)),
        out_shape=jax.ShapeDtypeStruct((6, FRAMES, lanes), f32),
        in_specs=[vmem, vmem],
        out_specs=vmem,
        scratch_shapes=[
            pltpu.VMEM((count // 2, 8, lanes), f32),
            pltpu.VMEM((count // 2, 8, lanes), f32),
            pltpu.VMEM((count, 8, lanes), f32),
            pltpu.VMEM((count // 2 + 1, 8, lanes), f32),
            pltpu.SMEM(words.shape, jnp.int32),
            pltpu.SemaphoreType.DMA((2,)),
            pltpu.SemaphoreType.DMA((2,)),
            pltpu.SemaphoreType.DMA,
        ],
        compiler_params=pltpu.CompilerParams(collective_id=1, has_side_effects=True, vmem_limit_bytes=20 * 1024 * 1024),
    )(grid.reshape(13 * LINES, 8, 128), words)


def local(positions, counts, plan, k_index):
    x, words, bounds = call_spread(plan, k_index, counts, positions)
    grid = call_lattice(bounds, x)
    factors = call_factors(grid, words, positions.shape[2] * lax.axis_size("atoms"))
    return jnp.transpose(factors, (1, 0, 2))


def solution(mesh):
    return jax.shard_map(
        local,
        mesh=mesh,
        in_specs=(P("ka", None, "atoms"), P("atoms", None), P(), P(None, "ka")),
        out_specs=P(None, None, "ka"),
        check_vma=False,
    )
```

```python
import functools
import math

import jax
import jax.numpy as jnp
import numpy as np
from jax import lax
from jax.experimental import pallas as pl
from jax.experimental.pallas import tpu as pltpu
from jax.sharding import PartitionSpec as P

MESH = pl.DeviceIdType.MESH
FRAMES = 8
LINES = 88
COARSE = 13
CHUNK = 256
GROUP = 4
BATCH = 16
HOPS = (0, 1, 2, 1)
ORDER = sorted(
    [(z, y, x, c) for c in range(2) for x in range(4) for y in range(4) for z in range(2) if z + y + x + c],
    key=lambda d: -(d[0] + HOPS[d[1]] + HOPS[d[2]]),
)
f32 = jnp.float32
bf16 = jnp.bfloat16

def fit_coefs():
    t = np.cos(np.pi * (np.arange(4000) + 0.5) / 4000) * 0.5
    u = t * t
    a = np.vander(u, 5, increasing=True)
    ps = np.linalg.lstsq(a * t[:, None], np.sin(np.pi * t), rcond=None)[0]
    pc = np.linalg.lstsq(a, np.cos(np.pi * t), rcond=None)[0]
    return [float(x) for x in ps], [float(x) for x in pc]

SIN_C, COS_C = fit_coefs()

def waves(cycles):
    t = cycles - jnp.round(cycles)
    u = t * t
    s = jnp.full_like(u, SIN_C[-1])
    for c in SIN_C[-2::-1]:
        s = s * u + c
    s = s * t
    q = jnp.full_like(u, COS_C[-1])
    for c in COS_C[-2::-1]:
        q = q * u + c
    twice = s + s
    return 1.0 - twice * s, twice * q

def split(x):
    hi = x.astype(bf16)
    lo = (x - hi.astype(f32)).astype(bf16)
    return hi, lo

def balanced(index, base, reach, mul, shift, below=0):
    upper = (((index + reach + base * below) * mul) >> shift) - below
    return upper, index - base * upper

def lattice_kernel(counts_ref, x_ref, grid, e01_a, e01_b, e2_a, e2_b, rhs_a, rhs_b, acc, counts, counts_sem):
    fetch = pltpu.make_async_copy(counts_ref, counts, counts_sem)
    fetch.start()
    me = lax.axis_index("ka")
    base = me - 2 * lax.rem(me // 2, FRAMES)
    acc[...] = jnp.zeros_like(acc)
    fetch.wait()
    pieces, _, rows, _ = x_ref.shape
    piece = rows * 128
    per_piece = piece // CHUNK
    chunks = pieces * per_piece
    end = [counts[0, 0], counts[0, 0] + counts[0, 1]]
    below = []
    for e in end:
        total = 0
        for p in range(pieces):
            total = total + jnp.clip(e - (base + 2 * p) * piece, 0, piece)
        below.append(total)
    cut0, cut1 = below
    turn0 = (cut0 + CHUNK - 1) // CHUNK
    turn1 = turn0 + (cut1 + CHUNK - 1) // CHUNK - cut0 // CHUNK
    visits = turn1 + chunks - cut1 // CHUNK

    lane = lax.broadcasted_iota(jnp.int32, (1, CHUNK), 1)

    def visit(v):
        kind = (v >= turn0).astype(jnp.int32) + (v >= turn1).astype(jnp.int32)
        chunk = jnp.where(kind == 0, v, jnp.where(kind == 1, v - turn0 + cut0 // CHUNK, v - turn1 + cut1 // CHUNK))
        first = jnp.where(kind == 0, 0, jnp.where(kind == 1, cut0, cut1))
        last = jnp.where(kind == 0, cut0, jnp.where(kind == 1, cut1, chunks * CHUNK))
        return kind, chunk, first, last

    def prepare(v, e01, e2, rhs):
        _, chunk, first, last = visit(v)
        here = jnp.minimum(chunk, chunks - 1)
        xs = []
        for d in range(3):
            at = lax.rem(here, per_piece) * (CHUNK // 128)
            parts = [x_ref[here // per_piece, d, pl.ds(at + n, 1)] for n in range(CHUNK // 128)]
            whole = jnp.concatenate(parts, axis=1)
            xs.append(whole - jnp.round(whole))
        where = chunk * CHUNK + lane
        mask = jnp.logical_and(where >= first, where < last).astype(f32)

        def lines(row):
            line = row + lax.broadcasted_iota(jnp.int32, (8, CHUNK), 0)
            q0, q1 = [(5 * q).astype(f32) for q in balanced(line, 13, 6, 79, 10)]
            c, s = waves(q0 * xs[0] + q1 * xs[1])
            e01[row:row + 8] = c
            e01[LINES + row:LINES + row + 8] = s

        def depths():
            q2 = (5 * lax.broadcasted_iota(jnp.int32, (8, CHUNK), 0)).astype(f32)
            c, s = waves(q2 * xs[2])
            e2[0:8] = c
            e2[8:16] = s

        def columns(row):
            index = row + lax.broadcasted_iota(jnp.int32, (16, CHUNK), 0)
            r0, rest = balanced(index, 25, 12, 41, 10)
            r1, r2 = balanced(rest, 5, 2, 205, 10, 3)
            c, s = waves(r0.astype(f32) * xs[0] + r1.astype(f32) * xs[1] + r2.astype(f32) * xs[2])
            for at, value in ((row, c), (64 + row, s)):
                hi, lo = split(value * mask)
                rhs[at:at + 16] = hi
                rhs[128 + at:144 + at] = lo

        steps = [functools.partial(lines, row) for row in range(0, LINES, 8)]
        steps += [functools.partial(columns, row) for row in range(0, 64, 16)]
        return steps + [depths]

    def gather(v, e01, e2, rhs, steps):
        kind = visit(v)[0]
        weights = rhs[...]
        for l in range(0, COARSE, 3):
            some = range(l, min(l + 3, COARSE))
            parts = []
            for m in some:
                row = m if m < 7 else m + 2
                parts += split(e01[...] * e2[row:row + 1])
            lhs = jnp.concatenate(parts, axis=0)
            p = lax.dot_general(lhs, weights, (((1,), (1,)), ((), ())), preferred_element_type=f32)
            for m in some:
                at = (m - l) * 4 * LINES
                one = p[at:at + 2 * LINES] + p[at + 2 * LINES:at + 4 * LINES]
                acc[kind, m] += one[:, :128] + one[:, 128:]
            for step in steps[l * len(steps) // COARSE:min(l + 3, COARSE) * len(steps) // COARSE]:
                step()

    buffers = ((e01_a, e2_a, rhs_a), (e01_b, e2_b, rhs_b))
    for step in prepare(0, *buffers[0]):
        step()

    def pair(i, _):
        gather(2 * i, *buffers[0], prepare(2 * i + 1, *buffers[1]))
        gather(2 * i + 1, *buffers[1], prepare(2 * i + 2, *buffers[0]))
        return 0

    lax.fori_loop(0, chunks // 2, pair, 0)

    @pl.when(visits > chunks)
    def _():
        gather(chunks, *buffers[0], [])

    @pl.when(visits > chunks + 1)
    def _():
        for step in prepare(chunks + 1, *buffers[1]):
            step()
        gather(chunks + 1, *buffers[1], [])

    front = lax.broadcasted_iota(jnp.int32, (LINES, 128), 1) < 64

    def put(q2, sp, a, b):
        plus = b + pltpu.roll(a, 64, axis=1)
        minus = a - pltpu.roll(b, 64, axis=1)
        at = (q2 + 6) * LINES * 8 + sp
        grid[pl.ds(at, LINES, stride=8), :] = jnp.where(front, minus, plus)
        grid[pl.ds(at + 4, LINES, stride=8), :] = jnp.where(front, plus, -minus)

    for sp in range(3):
        put(0, sp, acc[sp, 0, 0:LINES], acc[sp, 0, LINES:])
        for l in range(1, 7):
            cc, sc = acc[sp, l, 0:LINES], acc[sp, l, LINES:]
            cs, ss = acc[sp, l + 6, 0:LINES], acc[sp, l + 6, LINES:]
            put(l, sp, cc - ss, sc + cs)
            put(-l, sp, cc + ss, sc - cs)


def call_lattice(counts, x):
    vmem = pl.BlockSpec(memory_space=pltpu.VMEM)
    return pl.pallas_call(
        lattice_kernel,
        out_shape=jax.ShapeDtypeStruct((13 * LINES * 8, 128), f32),
        in_specs=[vmem, vmem],
        out_specs=vmem,
        scratch_shapes=[pltpu.VMEM((2 * LINES, CHUNK), f32)] * 2
        + [pltpu.VMEM((16, CHUNK), f32)] * 2
        + [pltpu.VMEM((256, CHUNK), bf16)] * 2
        + [pltpu.VMEM((3, COARSE, 2 * LINES, 128), f32), pltpu.SMEM(counts.shape, jnp.int32), pltpu.SemaphoreType.DMA],
        compiler_params=pltpu.CompilerParams(vmem_limit_bytes=24 * 1024 * 1024),
    )(counts, x)


def picks(k_index):
    n = [k_index[d:d + 1] for d in range(3)]
    q, r = zip(*[balanced(v, 5, 2, 205, 10, 6) for v in n])
    jc = 13 * q[0] + q[1]
    sq = jnp.where(jc < 0, 1, 0)
    tile = (jnp.where(jc < 0, -q[2], q[2]) + 6) * LINES + jnp.abs(jc)
    rc = 25 * r[0] + 5 * r[1] + r[2]
    sr = jnp.where(rc < 0, 1, 0)
    lane = lax.broadcasted_iota(jnp.int32, rc.shape, 1)
    shift = (lane - jnp.abs(rc) - 64 * (sr ^ sq)) & 127
    return tile * 256 + sq * 128 + shift


def spread_kernel(small_ref, pos_ref, x_ref, word_ref, bound_ref, slots, stage, plan, send_sem, recv_sem, own_sem):
    me = lax.axis_index("ka")
    count = lax.axis_size("ka")
    frame = lax.rem(me // 2, FRAMES)
    base = me - 2 * frame
    wide = 2 * FRAMES
    groups = count // FRAMES
    mine = me // wide * 2 + lax.rem(me, 2)
    barrier = pltpu.get_barrier_semaphore()
    fetches = [
        pltpu.make_async_copy(small_ref, plan, own_sem.at[0]),
        pltpu.make_async_copy(pos_ref.at[:, me], slots.at[me], own_sem.at[1]),
    ]
    for fetch in fetches:
        fetch.start()

    def greet(i, _):
        pl.semaphore_signal(barrier, inc=1, device_id={"ka": lax.rem(me + i, count)}, device_id_type=MESH)
        return 0

    lax.fori_loop(1, count, greet, 0)
    bound_ref[...] = small_ref[3:4]
    word_ref[mine, pl.ds(frame, 1)] = picks(small_ref[0:3])
    pl.semaphore_wait(barrier, count - 1)

    def share(i, _):
        to = lax.rem(frame + i, FRAMES)
        pltpu.make_async_remote_copy(
            src_ref=word_ref.at[mine, pl.ds(frame, 1)],
            dst_ref=word_ref.at[mine, pl.ds(frame, 1)],
            send_sem=send_sem.at[1],
            recv_sem=recv_sem.at[1],
            device_id={"ka": base + 2 * to},
            device_id_type=MESH,
        ).start()
        return 0

    lax.fori_loop(1, FRAMES, share, 0)

    z, y, x, core = me // 32, lax.rem(me // 8, 4), lax.rem(me // 2, 4), lax.rem(me, 2)
    for dz, dy, dx, dc in ORDER:
        to = lax.rem(z + dz, 2) * 32 + lax.rem(y + dy, 4) * 8 + lax.rem(x + dx, 4) * 2 + lax.rem(core + dc, 2)
        pltpu.make_async_remote_copy(
            src_ref=pos_ref.at[:, to],
            dst_ref=slots.at[me],
            send_sem=send_sem.at[0],
            recv_sem=recv_sem.at[0],
            device_id={"ka": to},
            device_id_type=MESH,
        ).start()
    row = word_ref.at[mine, pl.ds(0, FRAMES - 1)]
    pltpu.make_async_copy(row, row, recv_sem.at[1]).wait()

    def share_group(i, _):
        to = lax.rem(mine + i, groups)
        pltpu.make_async_remote_copy(
            src_ref=word_ref.at[mine],
            dst_ref=word_ref.at[mine],
            send_sem=send_sem.at[3],
            recv_sem=recv_sem.at[3],
            device_id={"ka": to // 2 * wide + 2 * frame + lax.rem(to, 2)},
            device_id_type=MESH,
        ).start()
        return 0

    lax.fori_loop(1, groups, share_group, 0)
    for fetch in fetches:
        fetch.wait()
    most = slots.at[pl.ds(0, count - 1)]
    pltpu.make_async_copy(most, most, recv_sem.at[0]).wait()
    for f in range(FRAMES):
        stage[f] = slots[plan[3, 8 + f]]

    def hand_on(i, _):
        to = lax.rem(frame + i, FRAMES)
        pltpu.make_async_remote_copy(
            src_ref=stage.at[to],
            dst_ref=x_ref.at[frame],
            send_sem=send_sem.at[2],
            recv_sem=recv_sem.at[2],
            device_id={"ka": base + 2 * to},
            device_id_type=MESH,
        ).start()
        return 0

    lax.fori_loop(1, FRAMES, hand_on, 0)
    x_ref[frame] = stage[frame]
    words = word_ref.at[pl.ds(0, groups - 1)]
    rest = x_ref.at[pl.ds(0, FRAMES - 1)]
    pltpu.make_async_copy(words, words, recv_sem.at[3]).wait()
    pltpu.make_async_copy(most, most, send_sem.at[0]).wait()
    pltpu.make_async_copy(row, row, send_sem.at[1]).wait()
    pltpu.make_async_copy(words, words, send_sem.at[3]).wait()
    pltpu.make_async_copy(rest, rest, recv_sem.at[2]).wait()
    pltpu.make_async_copy(rest, rest, send_sem.at[2]).wait()


def call_spread(plan, k_index, counts, positions):
    hbm = pl.BlockSpec(memory_space=pltpu.HBM)
    vmem = pl.BlockSpec(memory_space=pltpu.VMEM)
    count = lax.axis_size("ka")
    rows = positions.shape[2] // (128 * count)
    lanes = k_index.shape[1]
    small = jnp.pad(k_index, ((0, 1), (0, 0))) + jnp.pad(counts, ((3, 0), (0, lanes - 3))) + jnp.pad(plan[None], ((3, 0), (8, lanes - 16)))
    return pl.pallas_call(
        spread_kernel,
        out_shape=(
            jax.ShapeDtypeStruct((FRAMES, 3, rows, 128), f32),
            jax.ShapeDtypeStruct((count // FRAMES, FRAMES, lanes), jnp.int32),
            jax.ShapeDtypeStruct((1, lanes), jnp.int32),
        ),
        in_specs=[vmem, hbm],
        out_specs=(vmem, vmem, vmem),
        scratch_shapes=[
            pltpu.VMEM((count, 3, rows, 128), f32),
            pltpu.VMEM((FRAMES, 3, rows, 128), f32),
            pltpu.SMEM((4, lanes), jnp.int32),
            pltpu.SemaphoreType.DMA((4,)),
            pltpu.SemaphoreType.DMA((4,)),
            pltpu.SemaphoreType.DMA((2,)),
        ],
        compiler_params=pltpu.CompilerParams(collective_id=0, has_side_effects=True, vmem_limit_bytes=55000 * 1024),
    )(small, positions.reshape(3, count, rows, 128))


def pick_blocks(grid, pick, word_ref, modes, blocks, places):
    lanes = lax.broadcasted_iota(jnp.int32, (8, 128), 1)
    upper = lax.broadcasted_iota(jnp.int32, (8, 128), 0) < 4
    for b, at in zip(blocks, places):
        group, lead = b // (2 * FRAMES) * 2 + lax.rem(b, 2), lax.rem(b // 2, FRAMES)
        found = jnp.zeros((8, 128), f32)
        for j in range(128):
            word = pick[group, lead, j]
            found = jnp.where(lanes == j, pltpu.roll(grid[word >> 8], word & 127, axis=1), found)
        sign = jnp.where((word_ref[group, pl.ds(lead, 1)] & 128) > 0, -1.0, 1.0)
        modes[at] = found * jnp.where(upper, 1.0, sign)


def factors_kernel(scale, grid, word_ref, out_ref, modes, spare, parts, beside, pick, send_sem, recv_sem, own_sem):
    me = lax.axis_index("ka")
    half = lax.axis_index("atoms")
    chips = lax.axis_size("ka") // 2
    chip, core = me // 2, lax.rem(me, 2)
    barrier = pltpu.get_barrier_semaphore()
    fetch = pltpu.make_async_copy(word_ref, pick, own_sem)
    fetch.start()

    def greet(i, _):
        to = 2 * lax.rem(chip + i, chips) + core
        pl.semaphore_signal(barrier, inc=1, device_id={"ka": to, "atoms": 1 - half}, device_id_type=MESH)

        @pl.when(i < chips)
        def _():
            pl.semaphore_signal(barrier, inc=1, device_id={"ka": to, "atoms": half}, device_id_type=MESH)
        return 0

    pl.semaphore_signal(barrier, inc=1, device_id={"ka": 2 * chip + 1 - core}, device_id_type=MESH)
    lax.fori_loop(1, chips + 1, greet, 0)
    fetch.wait()
    slot = half * chips + chip

    def place(i):
        return lax.rem(chip + i + 1, chips)

    def hand_over(g):
        pltpu.make_async_remote_copy(
            src_ref=spare.at[pl.ds(BATCH * g, BATCH)],
            dst_ref=beside.at[pl.ds(BATCH * g, BATCH)],
            send_sem=send_sem.at[0],
            recv_sem=recv_sem.at[0],
            device_id={"ka": 2 * chip + 1 - core},
            device_id_type=MESH,
        ).start()

    def first_half(g, _):
        at = [BATCH * g + u for u in range(BATCH)]
        pick_blocks(grid, pick, word_ref, spare, [2 * place(i) + 1 - core for i in at], at)

        @pl.when(g == 1)
        def _():
            pl.semaphore_wait(barrier, 2 * chips)
            hand_over(0)

        @pl.when(g > 0)
        def _():
            hand_over(g)
        return 0

    lax.fori_loop(0, chips // BATCH, first_half, 0)
    handed = beside.at[pl.ds(0, chips)]

    def send(i):
        to = place(i)
        modes[i] += beside[i]

        def copy(h):
            return pltpu.make_async_remote_copy(
                src_ref=modes.at[i],
                dst_ref=parts.at[slot],
                send_sem=send_sem.at[1],
                recv_sem=recv_sem.at[1],
                device_id={"ka": 2 * to + core, "atoms": h},
                device_id_type=MESH,
            )

        copy(1 - half).start()

        @pl.when(i < chips - 1)
        def _():
            copy(half).start()

    def second_half(g, _):
        at = [GROUP * g + u for u in range(GROUP)]
        pick_blocks(grid, pick, word_ref, modes, [2 * place(i) + core for i in at], at)

        @pl.when(g == 1)
        def _():
            pltpu.make_async_copy(handed, handed, recv_sem.at[0]).wait()
            for u in range(GROUP):
                send(u)

        @pl.when(g > 0)
        def _():
            for i in at:
                send(i)
        return 0

    lax.fori_loop(0, chips // GROUP, second_half, 0)
    parts[slot] = modes[chips - 1]
    most = parts.at[pl.ds(0, 2 * chips - 1)]
    pltpu.make_async_copy(most, most, recv_sem.at[1]).wait()
    window = []
    for f in range(FRAMES):
        total = None
        for high in range(2 * chips // FRAMES):
            part = parts[high * FRAMES + f]
            total = part if total is None else total + part
        window.append(total)
    upper = lax.broadcasted_iota(jnp.int32, (8, 128), 0) < 4
    crossed = [jnp.where(upper, 1.0, -1.0) * pltpu.roll(w, 4, axis=0) for w in window]
    pairs = ((0, 0), (0, 1), (0, 2), (1, 1), (1, 2), (2, 2))
    for f in range(FRAMES):
        wave = window[0]
        for t in range(1, FRAMES):
            turn = 2 * math.pi * (f * t % FRAMES) / FRAMES
            wave = wave + math.cos(turn) * window[t] + math.sin(turn) * crossed[t]
        for p, (a, b) in enumerate(pairs):
            value = wave[a:a + 1] * wave[b:b + 1] + wave[4 + a:5 + a] * wave[4 + b:5 + b]
            out_ref[p, f:f + 1] = value * scale
    pltpu.make_async_copy(handed, handed, send_sem.at[0]).wait()
    pltpu.make_async_copy(most, most, send_sem.at[1]).wait()


def call_factors(grid, words, total_atoms):
    vmem = pl.BlockSpec(memory_space=pltpu.VMEM)
    count = lax.axis_size("ka")
    lanes = words.shape[2]
    return pl.pallas_call(
        functools.partial(factors_kernel, 1.0 / (FRAMES * total_atoms)),
        out_shape=jax.ShapeDtypeStruct((6, FRAMES, lanes), f32),
        in_specs=[vmem, vmem],
        out_specs=vmem,
        scratch_shapes=[
            pltpu.VMEM((count // 2, 8, lanes), f32),
            pltpu.VMEM((count // 2, 8, lanes), f32),
            pltpu.VMEM((count, 8, lanes), f32),
            pltpu.VMEM((count // 2 + 1, 8, lanes), f32),
            pltpu.SMEM(words.shape, jnp.int32),
            pltpu.SemaphoreType.DMA((2,)),
            pltpu.SemaphoreType.DMA((2,)),
            pltpu.SemaphoreType.DMA,
        ],
        compiler_params=pltpu.CompilerParams(collective_id=1, has_side_effects=True, vmem_limit_bytes=20 * 1024 * 1024),
    )(grid.reshape(13 * LINES, 8, 128), words)


def local(positions, counts, plan, k_index):
    x, words, bounds = call_spread(plan, k_index, counts, positions)
    grid = call_lattice(bounds, x)
    factors = call_factors(grid, words, positions.shape[2] * lax.axis_size("atoms"))
    return jnp.transpose(factors, (1, 0, 2))


def solution(mesh):
    return jax.shard_map(
        local,
        mesh=mesh,
        in_specs=(P("ka", None, "atoms"), P("atoms", None), P(), P(None, "ka")),
        out_specs=P(None, None, "ka"),
        check_vma=False,
    )
```

```python
import functools
import math

import jax
import jax.numpy as jnp
import numpy as np
from jax import lax
from jax.experimental import pallas as pl
from jax.experimental.pallas import tpu as pltpu
from jax.sharding import PartitionSpec as P

MESH = pl.DeviceIdType.MESH
FRAMES = 8
LINES = 88
COARSE = 13
CHUNK = 256
STRETCHES = (14, 10, 5, 3)
BATCH = 16
HOPS = (0, 1, 2, 1)
ORDER = sorted(
    [(z, y, x, c) for c in range(2) for x in range(4) for y in range(4) for z in range(2) if z + y + x + c],
    key=lambda d: -(d[0] + HOPS[d[1]] + HOPS[d[2]]),
)
f32 = jnp.float32
bf16 = jnp.bfloat16

def fit_coefs():
    t = np.cos(np.pi * (np.arange(4000) + 0.5) / 4000) * 0.5
    u = t * t
    a = np.vander(u, 5, increasing=True)
    ps = np.linalg.lstsq(a * t[:, None], np.sin(np.pi * t), rcond=None)[0]
    pc = np.linalg.lstsq(a, np.cos(np.pi * t), rcond=None)[0]
    return [float(x) for x in ps], [float(x) for x in pc]

SIN_C, COS_C = fit_coefs()

def waves(cycles):
    t = cycles - jnp.round(cycles)
    u = t * t
    s = jnp.full_like(u, SIN_C[-1])
    for c in SIN_C[-2::-1]:
        s = s * u + c
    s = s * t
    q = jnp.full_like(u, COS_C[-1])
    for c in COS_C[-2::-1]:
        q = q * u + c
    twice = s + s
    return 1.0 - twice * s, twice * q

def split(x):
    hi = x.astype(bf16)
    lo = (x - hi.astype(f32)).astype(bf16)
    return hi, lo

def balanced(index, base, reach, mul, shift, below=0):
    upper = (((index + reach + base * below) * mul) >> shift) - below
    return upper, index - base * upper

def lattice_kernel(counts_ref, x_ref, grid, e01_a, e01_b, e2_a, e2_b, rhs_a, rhs_b, acc, counts, counts_sem):
    fetch = pltpu.make_async_copy(counts_ref, counts, counts_sem)
    fetch.start()
    me = lax.axis_index("ka")
    base = me - 2 * lax.rem(me // 2, FRAMES)
    acc[...] = jnp.zeros_like(acc)
    fetch.wait()
    pieces, _, rows, _ = x_ref.shape
    piece = rows * 128
    per_piece = piece // CHUNK
    chunks = pieces * per_piece
    end = [counts[0, 0], counts[0, 0] + counts[0, 1]]
    below = []
    for e in end:
        total = 0
        for p in range(pieces):
            total = total + jnp.clip(e - (base + 2 * p) * piece, 0, piece)
        below.append(total)
    cut0, cut1 = below
    turn0 = (cut0 + CHUNK - 1) // CHUNK
    turn1 = turn0 + (cut1 + CHUNK - 1) // CHUNK - cut0 // CHUNK
    visits = turn1 + chunks - cut1 // CHUNK

    lane = lax.broadcasted_iota(jnp.int32, (1, CHUNK), 1)

    def visit(v):
        kind = (v >= turn0).astype(jnp.int32) + (v >= turn1).astype(jnp.int32)
        chunk = jnp.where(kind == 0, v, jnp.where(kind == 1, v - turn0 + cut0 // CHUNK, v - turn1 + cut1 // CHUNK))
        first = jnp.where(kind == 0, 0, jnp.where(kind == 1, cut0, cut1))
        last = jnp.where(kind == 0, cut0, jnp.where(kind == 1, cut1, chunks * CHUNK))
        return kind, chunk, first, last

    def prepare(v, e01, e2, rhs):
        _, chunk, first, last = visit(v)
        here = jnp.minimum(chunk, chunks - 1)
        xs = []
        for d in range(3):
            at = lax.rem(here, per_piece) * (CHUNK // 128)
            parts = [x_ref[here // per_piece, d, pl.ds(at + n, 1)] for n in range(CHUNK // 128)]
            whole = jnp.concatenate(parts, axis=1)
            xs.append(whole - jnp.round(whole))
        where = chunk * CHUNK + lane
        mask = jnp.logical_and(where >= first, where < last).astype(f32)

        def lines(row):
            line = row + lax.broadcasted_iota(jnp.int32, (8, CHUNK), 0)
            q0, q1 = [(5 * q).astype(f32) for q in balanced(line, 13, 6, 79, 10)]
            c, s = waves(q0 * xs[0] + q1 * xs[1])
            e01[row:row + 8] = c
            e01[LINES + row:LINES + row + 8] = s

        def depths():
            q2 = (5 * lax.broadcasted_iota(jnp.int32, (8, CHUNK), 0)).astype(f32)
            c, s = waves(q2 * xs[2])
            e2[0:8] = c
            e2[8:16] = s

        def columns(row):
            index = row + lax.broadcasted_iota(jnp.int32, (16, CHUNK), 0)
            r0, rest = balanced(index, 25, 12, 41, 10)
            r1, r2 = balanced(rest, 5, 2, 205, 10, 3)
            c, s = waves(r0.astype(f32) * xs[0] + r1.astype(f32) * xs[1] + r2.astype(f32) * xs[2])
            for at, value in ((row, c), (64 + row, s)):
                hi, lo = split(value * mask)
                rhs[at:at + 16] = hi
                rhs[128 + at:144 + at] = lo

        steps = [functools.partial(lines, row) for row in range(0, LINES, 8)]
        steps += [functools.partial(columns, row) for row in range(0, 64, 16)]
        return steps + [depths]

    def gather(v, e01, e2, rhs, steps):
        kind = visit(v)[0]
        weights = rhs[...]
        for l in range(0, COARSE, 3):
            some = range(l, min(l + 3, COARSE))
            parts = []
            for m in some:
                row = m if m < 7 else m + 2
                parts += split(e01[...] * e2[row:row + 1])
            lhs = jnp.concatenate(parts, axis=0)
            p = lax.dot_general(lhs, weights, (((1,), (1,)), ((), ())), preferred_element_type=f32)
            for m in some:
                at = (m - l) * 4 * LINES
                one = p[at:at + 2 * LINES] + p[at + 2 * LINES:at + 4 * LINES]
                acc[kind, m] += one[:, :128] + one[:, 128:]
            for step in steps[l * len(steps) // COARSE:min(l + 3, COARSE) * len(steps) // COARSE]:
                step()

    buffers = ((e01_a, e2_a, rhs_a), (e01_b, e2_b, rhs_b))
    for step in prepare(0, *buffers[0]):
        step()

    def pair(i, _):
        gather(2 * i, *buffers[0], prepare(2 * i + 1, *buffers[1]))
        gather(2 * i + 1, *buffers[1], prepare(2 * i + 2, *buffers[0]))
        return 0

    lax.fori_loop(0, chunks // 2, pair, 0)

    @pl.when(visits > chunks)
    def _():
        gather(chunks, *buffers[0], [])

    @pl.when(visits > chunks + 1)
    def _():
        for step in prepare(chunks + 1, *buffers[1]):
            step()
        gather(chunks + 1, *buffers[1], [])

    front = lax.broadcasted_iota(jnp.int32, (LINES, 128), 1) < 64

    def put(q2, sp, a, b):
        plus = b + pltpu.roll(a, 64, axis=1)
        minus = a - pltpu.roll(b, 64, axis=1)
        at = (q2 + 6) * LINES * 8 + sp
        grid[pl.ds(at, LINES, stride=8), :] = jnp.where(front, minus, plus)
        grid[pl.ds(at + 4, LINES, stride=8), :] = jnp.where(front, plus, -minus)

    for sp in range(3):
        put(0, sp, acc[sp, 0, 0:LINES], acc[sp, 0, LINES:])
        for l in range(1, 7):
            cc, sc = acc[sp, l, 0:LINES], acc[sp, l, LINES:]
            cs, ss = acc[sp, l + 6, 0:LINES], acc[sp, l + 6, LINES:]
            put(l, sp, cc - ss, sc + cs)
            put(-l, sp, cc + ss, sc - cs)


def call_lattice(counts, x):
    vmem = pl.BlockSpec(memory_space=pltpu.VMEM)
    return pl.pallas_call(
        lattice_kernel,
        out_shape=jax.ShapeDtypeStruct((13 * LINES * 8, 128), f32),
        in_specs=[vmem, vmem],
        out_specs=vmem,
        scratch_shapes=[pltpu.VMEM((2 * LINES, CHUNK), f32)] * 2
        + [pltpu.VMEM((16, CHUNK), f32)] * 2
        + [pltpu.VMEM((256, CHUNK), bf16)] * 2
        + [pltpu.VMEM((3, COARSE, 2 * LINES, 128), f32), pltpu.SMEM(counts.shape, jnp.int32), pltpu.SemaphoreType.DMA],
        compiler_params=pltpu.CompilerParams(vmem_limit_bytes=24 * 1024 * 1024),
    )(counts, x)


def picks(k_index):
    n = [k_index[d:d + 1] for d in range(3)]
    q, r = zip(*[balanced(v, 5, 2, 205, 10, 6) for v in n])
    jc = 13 * q[0] + q[1]
    sq = jnp.where(jc < 0, 1, 0)
    tile = (jnp.where(jc < 0, -q[2], q[2]) + 6) * LINES + jnp.abs(jc)
    rc = 25 * r[0] + 5 * r[1] + r[2]
    sr = jnp.where(rc < 0, 1, 0)
    lane = lax.broadcasted_iota(jnp.int32, rc.shape, 1)
    shift = (lane - jnp.abs(rc) - 64 * (sr ^ sq)) & 127
    return tile * 256 + sq * 128 + shift


def spread_kernel(small_ref, pos_ref, x_ref, word_ref, bound_ref, slots, stage, plan, send_sem, recv_sem, own_sem):
    me = lax.axis_index("ka")
    count = lax.axis_size("ka")
    frame = lax.rem(me // 2, FRAMES)
    base = me - 2 * frame
    wide = 2 * FRAMES
    groups = count // FRAMES
    mine = me // wide * 2 + lax.rem(me, 2)
    barrier = pltpu.get_barrier_semaphore()
    fetches = [
        pltpu.make_async_copy(small_ref, plan, own_sem.at[0]),
        pltpu.make_async_copy(pos_ref.at[:, me], slots.at[me], own_sem.at[1]),
    ]
    for fetch in fetches:
        fetch.start()

    def greet(i, _):
        pl.semaphore_signal(barrier, inc=1, device_id={"ka": lax.rem(me + i, count)}, device_id_type=MESH)
        return 0

    lax.fori_loop(1, count, greet, 0)
    bound_ref[...] = small_ref[3:4]
    word_ref[mine, pl.ds(frame, 1)] = picks(small_ref[0:3])
    pl.semaphore_wait(barrier, count - 1)

    def share(i, _):
        to = lax.rem(frame + i, FRAMES)
        pltpu.make_async_remote_copy(
            src_ref=word_ref.at[mine, pl.ds(frame, 1)],
            dst_ref=word_ref.at[mine, pl.ds(frame, 1)],
            send_sem=send_sem.at[1],
            recv_sem=recv_sem.at[1],
            device_id={"ka": base + 2 * to},
            device_id_type=MESH,
        ).start()
        return 0

    lax.fori_loop(1, FRAMES, share, 0)

    z, y, x, core = me // 32, lax.rem(me // 8, 4), lax.rem(me // 2, 4), lax.rem(me, 2)
    for dz, dy, dx, dc in ORDER:
        to = lax.rem(z + dz, 2) * 32 + lax.rem(y + dy, 4) * 8 + lax.rem(x + dx, 4) * 2 + lax.rem(core + dc, 2)
        pltpu.make_async_remote_copy(
            src_ref=pos_ref.at[:, to],
            dst_ref=slots.at[me],
            send_sem=send_sem.at[0],
            recv_sem=recv_sem.at[0],
            device_id={"ka": to},
            device_id_type=MESH,
        ).start()
    row = word_ref.at[mine, pl.ds(0, FRAMES - 1)]
    pltpu.make_async_copy(row, row, recv_sem.at[1]).wait()

    def share_group(i, _):
        to = lax.rem(mine + i, groups)
        pltpu.make_async_remote_copy(
            src_ref=word_ref.at[mine],
            dst_ref=word_ref.at[mine],
            send_sem=send_sem.at[3],
            recv_sem=recv_sem.at[3],
            device_id={"ka": to // 2 * wide + 2 * frame + lax.rem(to, 2)},
            device_id_type=MESH,
        ).start()
        return 0

    lax.fori_loop(1, groups, share_group, 0)
    for fetch in fetches:
        fetch.wait()
    most = slots.at[pl.ds(0, count - 1)]
    pltpu.make_async_copy(most, most, recv_sem.at[0]).wait()
    for f in range(FRAMES):
        stage[f] = slots[plan[3, 8 + f]]

    def hand_on(i, _):
        to = lax.rem(frame + i, FRAMES)
        pltpu.make_async_remote_copy(
            src_ref=stage.at[to],
            dst_ref=x_ref.at[frame],
            send_sem=send_sem.at[2],
            recv_sem=recv_sem.at[2],
            device_id={"ka": base + 2 * to},
            device_id_type=MESH,
        ).start()
        return 0

    lax.fori_loop(1, FRAMES, hand_on, 0)
    x_ref[frame] = stage[frame]
    words = word_ref.at[pl.ds(0, groups - 1)]
    rest = x_ref.at[pl.ds(0, FRAMES - 1)]
    pltpu.make_async_copy(words, words, recv_sem.at[3]).wait()
    pltpu.make_async_copy(most, most, send_sem.at[0]).wait()
    pltpu.make_async_copy(row, row, send_sem.at[1]).wait()
    pltpu.make_async_copy(words, words, send_sem.at[3]).wait()
    pltpu.make_async_copy(rest, rest, recv_sem.at[2]).wait()
    pltpu.make_async_copy(rest, rest, send_sem.at[2]).wait()


def call_spread(plan, k_index, counts, positions):
    hbm = pl.BlockSpec(memory_space=pltpu.HBM)
    vmem = pl.BlockSpec(memory_space=pltpu.VMEM)
    count = lax.axis_size("ka")
    rows = positions.shape[2] // (128 * count)
    lanes = k_index.shape[1]
    small = jnp.pad(k_index, ((0, 1), (0, 0))) + jnp.pad(counts, ((3, 0), (0, lanes - 3))) + jnp.pad(plan[None], ((3, 0), (8, lanes - 16)))
    return pl.pallas_call(
        spread_kernel,
        out_shape=(
            jax.ShapeDtypeStruct((FRAMES, 3, rows, 128), f32),
            jax.ShapeDtypeStruct((count // FRAMES, FRAMES, lanes), jnp.int32),
            jax.ShapeDtypeStruct((1, lanes), jnp.int32),
        ),
        in_specs=[vmem, hbm],
        out_specs=(vmem, vmem, vmem),
        scratch_shapes=[
            pltpu.VMEM((count, 3, rows, 128), f32),
            pltpu.VMEM((FRAMES, 3, rows, 128), f32),
            pltpu.SMEM((4, lanes), jnp.int32),
            pltpu.SemaphoreType.DMA((4,)),
            pltpu.SemaphoreType.DMA((4,)),
            pltpu.SemaphoreType.DMA((2,)),
        ],
        compiler_params=pltpu.CompilerParams(collective_id=0, has_side_effects=True, vmem_limit_bytes=55000 * 1024),
    )(small, positions.reshape(3, count, rows, 128))


def pick_blocks(grid, pick, word_ref, modes, blocks, places):
    lanes = lax.broadcasted_iota(jnp.int32, (8, 128), 1)
    upper = lax.broadcasted_iota(jnp.int32, (8, 128), 0) < 4
    for b, at in zip(blocks, places):
        group, lead = b // (2 * FRAMES) * 2 + lax.rem(b, 2), lax.rem(b // 2, FRAMES)
        found = jnp.zeros((8, 128), f32)
        for j in range(128):
            word = pick[group, lead, j]
            found = jnp.where(lanes == j, pltpu.roll(grid[word >> 8], word & 127, axis=1), found)
        sign = jnp.where((word_ref[group, pl.ds(lead, 1)] & 128) > 0, -1.0, 1.0)
        modes[at] = found * jnp.where(upper, 1.0, sign)


def factors_kernel(scale, grid, word_ref, out_ref, modes, spare, parts, beside, pick, send_sem, recv_sem, own_sem):
    me = lax.axis_index("ka")
    half = lax.axis_index("atoms")
    chips = lax.axis_size("ka") // 2
    chip, core = me // 2, lax.rem(me, 2)
    barrier = pltpu.get_barrier_semaphore()
    fetch = pltpu.make_async_copy(word_ref, pick, own_sem)
    fetch.start()

    def greet(i, _):
        to = 2 * lax.rem(chip + i, chips) + core
        pl.semaphore_signal(barrier, inc=1, device_id={"ka": to, "atoms": 1 - half}, device_id_type=MESH)

        @pl.when(i < chips)
        def _():
            pl.semaphore_signal(barrier, inc=1, device_id={"ka": to, "atoms": half}, device_id_type=MESH)
        return 0

    pl.semaphore_signal(barrier, inc=1, device_id={"ka": 2 * chip + 1 - core}, device_id_type=MESH)
    lax.fori_loop(1, chips + 1, greet, 0)
    fetch.wait()
    slot = half * chips + chip

    def place(i):
        return lax.rem(chip + i + 1, chips)

    def hand_over(g):
        pltpu.make_async_remote_copy(
            src_ref=spare.at[pl.ds(BATCH * g, BATCH)],
            dst_ref=beside.at[pl.ds(BATCH * g, BATCH)],
            send_sem=send_sem.at[0],
            recv_sem=recv_sem.at[0],
            device_id={"ka": 2 * chip + 1 - core},
            device_id_type=MESH,
        ).start()

    def first_half(g, _):
        at = [BATCH * g + u for u in range(BATCH)]
        pick_blocks(grid, pick, word_ref, spare, [2 * place(i) + 1 - core for i in at], at)

        @pl.when(g == 1)
        def _():
            pl.semaphore_wait(barrier, 2 * chips)
            hand_over(0)

        @pl.when(g > 0)
        def _():
            hand_over(g)
        return 0

    lax.fori_loop(0, chips // BATCH, first_half, 0)
    handed = beside.at[pl.ds(0, chips)]

    def send(i):
        to = place(i)
        modes[i] += beside[i]

        def copy(h):
            return pltpu.make_async_remote_copy(
                src_ref=modes.at[i],
                dst_ref=parts.at[slot],
                send_sem=send_sem.at[1],
                recv_sem=recv_sem.at[1],
                device_id={"ka": 2 * to + core, "atoms": h},
                device_id_type=MESH,
            )

        copy(1 - half).start()

        @pl.when(i < chips - 1)
        def _():
            copy(half).start()

    def send_next(i, _):
        send(i)
        return 0

    start = 0
    for size in STRETCHES:
        at = list(range(start, start + size))
        pick_blocks(grid, pick, word_ref, modes, [2 * place(i) + core for i in at], at)
        if start == 0:
            pltpu.make_async_copy(handed, handed, recv_sem.at[0]).wait()
        lax.fori_loop(start, start + size, send_next, 0)
        start += size
    parts[slot] = modes[chips - 1]
    most = parts.at[pl.ds(0, 2 * chips - 1)]
    pltpu.make_async_copy(most, most, recv_sem.at[1]).wait()
    window = []
    for f in range(FRAMES):
        total = None
        for high in range(2 * chips // FRAMES):
            part = parts[high * FRAMES + f]
            total = part if total is None else total + part
        window.append(total)
    upper = lax.broadcasted_iota(jnp.int32, (8, 128), 0) < 4
    crossed = [jnp.where(upper, 1.0, -1.0) * pltpu.roll(w, 4, axis=0) for w in window]
    pairs = ((0, 0), (0, 1), (0, 2), (1, 1), (1, 2), (2, 2))
    for f in range(FRAMES):
        wave = window[0]
        for t in range(1, FRAMES):
            turn = 2 * math.pi * (f * t % FRAMES) / FRAMES
            wave = wave + math.cos(turn) * window[t] + math.sin(turn) * crossed[t]
        for p, (a, b) in enumerate(pairs):
            value = wave[a:a + 1] * wave[b:b + 1] + wave[4 + a:5 + a] * wave[4 + b:5 + b]
            out_ref[p, f:f + 1] = value * scale
    pltpu.make_async_copy(handed, handed, send_sem.at[0]).wait()
    pltpu.make_async_copy(most, most, send_sem.at[1]).wait()


def call_factors(grid, words, total_atoms):
    vmem = pl.BlockSpec(memory_space=pltpu.VMEM)
    count = lax.axis_size("ka")
    lanes = words.shape[2]
    return pl.pallas_call(
        functools.partial(factors_kernel, 1.0 / (FRAMES * total_atoms)),
        out_shape=jax.ShapeDtypeStruct((6, FRAMES, lanes), f32),
        in_specs=[vmem, vmem],
        out_specs=vmem,
        scratch_shapes=[
            pltpu.VMEM((count // 2, 8, lanes), f32),
            pltpu.VMEM((count // 2, 8, lanes), f32),
            pltpu.VMEM((count, 8, lanes), f32),
            pltpu.VMEM((count // 2 + 1, 8, lanes), f32),
            pltpu.SMEM(words.shape, jnp.int32),
            pltpu.SemaphoreType.DMA((2,)),
            pltpu.SemaphoreType.DMA((2,)),
            pltpu.SemaphoreType.DMA,
        ],
        compiler_params=pltpu.CompilerParams(collective_id=1, has_side_effects=True, vmem_limit_bytes=20 * 1024 * 1024),
    )(grid.reshape(13 * LINES, 8, 128), words)


def local(positions, counts, plan, k_index):
    x, words, bounds = call_spread(plan, k_index, counts, positions)
    grid = call_lattice(bounds, x)
    factors = call_factors(grid, words, positions.shape[2] * lax.axis_size("atoms"))
    return jnp.transpose(factors, (1, 0, 2))


def solution(mesh):
    return jax.shard_map(
        local,
        mesh=mesh,
        in_specs=(P("ka", None, "atoms"), P("atoms", None), P(), P(None, "ka")),
        out_specs=P(None, None, "ka"),
        check_vma=False,
    )
```

```python
import functools
import math

import jax
import jax.numpy as jnp
import numpy as np
from jax import lax
from jax.experimental import pallas as pl
from jax.experimental.pallas import tpu as pltpu
from jax.sharding import PartitionSpec as P

MESH = pl.DeviceIdType.MESH
FRAMES = 8
LINES = 88
COARSE = 13
CHUNK = 256
STRETCHES = (16, 9, 5, 2)
BATCH = 16
HOPS = (0, 1, 2, 1)
ORDER = sorted(
    [(z, y, x, c) for c in range(2) for x in range(4) for y in range(4) for z in range(2) if z + y + x + c],
    key=lambda d: -(d[0] + HOPS[d[1]] + HOPS[d[2]]),
)
f32 = jnp.float32
bf16 = jnp.bfloat16

def fit_coefs():
    t = np.cos(np.pi * (np.arange(4000) + 0.5) / 4000) * 0.5
    u = t * t
    a = np.vander(u, 5, increasing=True)
    ps = np.linalg.lstsq(a * t[:, None], np.sin(np.pi * t), rcond=None)[0]
    pc = np.linalg.lstsq(a, np.cos(np.pi * t), rcond=None)[0]
    return [float(x) for x in ps], [float(x) for x in pc]

SIN_C, COS_C = fit_coefs()

def waves(cycles):
    t = cycles - jnp.round(cycles)
    u = t * t
    s = jnp.full_like(u, SIN_C[-1])
    for c in SIN_C[-2::-1]:
        s = s * u + c
    s = s * t
    q = jnp.full_like(u, COS_C[-1])
    for c in COS_C[-2::-1]:
        q = q * u + c
    twice = s + s
    return 1.0 - twice * s, twice * q

def split(x):
    hi = x.astype(bf16)
    lo = (x - hi.astype(f32)).astype(bf16)
    return hi, lo

def balanced(index, base, reach, mul, shift, below=0):
    upper = (((index + reach + base * below) * mul) >> shift) - below
    return upper, index - base * upper

def lattice_kernel(counts_ref, x_ref, grid, e01_a, e01_b, e2_a, e2_b, rhs_a, rhs_b, acc, counts, counts_sem):
    fetch = pltpu.make_async_copy(counts_ref, counts, counts_sem)
    fetch.start()
    me = lax.axis_index("ka")
    base = me - 2 * lax.rem(me // 2, FRAMES)
    acc[...] = jnp.zeros_like(acc)
    fetch.wait()
    pieces, _, rows, _ = x_ref.shape
    piece = rows * 128
    per_piece = piece // CHUNK
    chunks = pieces * per_piece
    end = [counts[0, 0], counts[0, 0] + counts[0, 1]]
    below = []
    for e in end:
        total = 0
        for p in range(pieces):
            total = total + jnp.clip(e - (base + 2 * p) * piece, 0, piece)
        below.append(total)
    cut0, cut1 = below
    turn0 = (cut0 + CHUNK - 1) // CHUNK
    turn1 = turn0 + (cut1 + CHUNK - 1) // CHUNK - cut0 // CHUNK
    visits = turn1 + chunks - cut1 // CHUNK

    lane = lax.broadcasted_iota(jnp.int32, (1, CHUNK), 1)

    def visit(v):
        kind = (v >= turn0).astype(jnp.int32) + (v >= turn1).astype(jnp.int32)
        chunk = jnp.where(kind == 0, v, jnp.where(kind == 1, v - turn0 + cut0 // CHUNK, v - turn1 + cut1 // CHUNK))
        first = jnp.where(kind == 0, 0, jnp.where(kind == 1, cut0, cut1))
        last = jnp.where(kind == 0, cut0, jnp.where(kind == 1, cut1, chunks * CHUNK))
        return kind, chunk, first, last

    def prepare(v, e01, e2, rhs):
        _, chunk, first, last = visit(v)
        here = jnp.minimum(chunk, chunks - 1)
        xs = []
        for d in range(3):
            at = lax.rem(here, per_piece) * (CHUNK // 128)
            parts = [x_ref[here // per_piece, d, pl.ds(at + n, 1)] for n in range(CHUNK // 128)]
            whole = jnp.concatenate(parts, axis=1)
            xs.append(whole - jnp.round(whole))
        where = chunk * CHUNK + lane
        mask = jnp.logical_and(where >= first, where < last).astype(f32)

        def lines(row):
            line = row + lax.broadcasted_iota(jnp.int32, (8, CHUNK), 0)
            q0, q1 = [(5 * q).astype(f32) for q in balanced(line, 13, 6, 79, 10)]
            c, s = waves(q0 * xs[0] + q1 * xs[1])
            e01[row:row + 8] = c
            e01[LINES + row:LINES + row + 8] = s

        def depths():
            q2 = (5 * lax.broadcasted_iota(jnp.int32, (8, CHUNK), 0)).astype(f32)
            c, s = waves(q2 * xs[2])
            e2[0:8] = c
            e2[8:16] = s

        def columns(row):
            index = row + lax.broadcasted_iota(jnp.int32, (16, CHUNK), 0)
            r0, rest = balanced(index, 25, 12, 41, 10)
            r1, r2 = balanced(rest, 5, 2, 205, 10, 3)
            c, s = waves(r0.astype(f32) * xs[0] + r1.astype(f32) * xs[1] + r2.astype(f32) * xs[2])
            for at, value in ((row, c), (64 + row, s)):
                hi, lo = split(value * mask)
                rhs[at:at + 16] = hi
                rhs[128 + at:144 + at] = lo

        steps = [functools.partial(lines, row) for row in range(0, LINES, 8)]
        steps += [functools.partial(columns, row) for row in range(0, 64, 16)]
        return steps + [depths]

    def gather(v, e01, e2, rhs, steps):
        kind = visit(v)[0]
        weights = rhs[...]
        for l in range(0, COARSE, 3):
            some = range(l, min(l + 3, COARSE))
            parts = []
            for m in some:
                row = m if m < 7 else m + 2
                parts += split(e01[...] * e2[row:row + 1])
            lhs = jnp.concatenate(parts, axis=0)
            p = lax.dot_general(lhs, weights, (((1,), (1,)), ((), ())), preferred_element_type=f32)
            for m in some:
                at = (m - l) * 4 * LINES
                one = p[at:at + 2 * LINES] + p[at + 2 * LINES:at + 4 * LINES]
                acc[kind, m] += one[:, :128] + one[:, 128:]
            for step in steps[l * len(steps) // COARSE:min(l + 3, COARSE) * len(steps) // COARSE]:
                step()

    buffers = ((e01_a, e2_a, rhs_a), (e01_b, e2_b, rhs_b))
    for step in prepare(0, *buffers[0]):
        step()

    def pair(i, _):
        gather(2 * i, *buffers[0], prepare(2 * i + 1, *buffers[1]))
        gather(2 * i + 1, *buffers[1], prepare(2 * i + 2, *buffers[0]))
        return 0

    lax.fori_loop(0, chunks // 2, pair, 0)

    @pl.when(visits > chunks)
    def _():
        gather(chunks, *buffers[0], [])

    @pl.when(visits > chunks + 1)
    def _():
        for step in prepare(chunks + 1, *buffers[1]):
            step()
        gather(chunks + 1, *buffers[1], [])

    front = lax.broadcasted_iota(jnp.int32, (LINES, 128), 1) < 64

    def put(q2, sp, a, b):
        plus = b + pltpu.roll(a, 64, axis=1)
        minus = a - pltpu.roll(b, 64, axis=1)
        at = (q2 + 6) * LINES * 8 + sp
        grid[pl.ds(at, LINES, stride=8), :] = jnp.where(front, minus, plus)
        grid[pl.ds(at + 4, LINES, stride=8), :] = jnp.where(front, plus, -minus)

    for sp in range(3):
        put(0, sp, acc[sp, 0, 0:LINES], acc[sp, 0, LINES:])
        for l in range(1, 7):
            cc, sc = acc[sp, l, 0:LINES], acc[sp, l, LINES:]
            cs, ss = acc[sp, l + 6, 0:LINES], acc[sp, l + 6, LINES:]
            put(l, sp, cc - ss, sc + cs)
            put(-l, sp, cc + ss, sc - cs)


def call_lattice(counts, x):
    vmem = pl.BlockSpec(memory_space=pltpu.VMEM)
    return pl.pallas_call(
        lattice_kernel,
        out_shape=jax.ShapeDtypeStruct((13 * LINES * 8, 128), f32),
        in_specs=[vmem, vmem],
        out_specs=vmem,
        scratch_shapes=[pltpu.VMEM((2 * LINES, CHUNK), f32)] * 2
        + [pltpu.VMEM((16, CHUNK), f32)] * 2
        + [pltpu.VMEM((256, CHUNK), bf16)] * 2
        + [pltpu.VMEM((3, COARSE, 2 * LINES, 128), f32), pltpu.SMEM(counts.shape, jnp.int32), pltpu.SemaphoreType.DMA],
        compiler_params=pltpu.CompilerParams(vmem_limit_bytes=24 * 1024 * 1024),
    )(counts, x)


def picks(k_index):
    n = [k_index[d:d + 1] for d in range(3)]
    q, r = zip(*[balanced(v, 5, 2, 205, 10, 6) for v in n])
    jc = 13 * q[0] + q[1]
    sq = jnp.where(jc < 0, 1, 0)
    tile = (jnp.where(jc < 0, -q[2], q[2]) + 6) * LINES + jnp.abs(jc)
    rc = 25 * r[0] + 5 * r[1] + r[2]
    sr = jnp.where(rc < 0, 1, 0)
    lane = lax.broadcasted_iota(jnp.int32, rc.shape, 1)
    shift = (lane - jnp.abs(rc) - 64 * (sr ^ sq)) & 127
    return tile * 256 + sq * 128 + shift


def spread_kernel(small_ref, pos_ref, x_ref, word_ref, bound_ref, slots, stage, plan, send_sem, recv_sem, own_sem):
    me = lax.axis_index("ka")
    count = lax.axis_size("ka")
    frame = lax.rem(me // 2, FRAMES)
    base = me - 2 * frame
    wide = 2 * FRAMES
    groups = count // FRAMES
    mine = me // wide * 2 + lax.rem(me, 2)
    barrier = pltpu.get_barrier_semaphore()
    fetches = [
        pltpu.make_async_copy(small_ref, plan, own_sem.at[0]),
        pltpu.make_async_copy(pos_ref.at[:, me], slots.at[me], own_sem.at[1]),
    ]
    for fetch in fetches:
        fetch.start()

    def greet(i, _):
        pl.semaphore_signal(barrier, inc=1, device_id={"ka": lax.rem(me + i, count)}, device_id_type=MESH)
        return 0

    lax.fori_loop(1, count, greet, 0)
    bound_ref[...] = small_ref[3:4]
    word_ref[mine, pl.ds(frame, 1)] = picks(small_ref[0:3])
    pl.semaphore_wait(barrier, count - 1)

    def share(i, _):
        to = lax.rem(frame + i, FRAMES)
        pltpu.make_async_remote_copy(
            src_ref=word_ref.at[mine, pl.ds(frame, 1)],
            dst_ref=word_ref.at[mine, pl.ds(frame, 1)],
            send_sem=send_sem.at[1],
            recv_sem=recv_sem.at[1],
            device_id={"ka": base + 2 * to},
            device_id_type=MESH,
        ).start()
        return 0

    lax.fori_loop(1, FRAMES, share, 0)

    z, y, x, core = me // 32, lax.rem(me // 8, 4), lax.rem(me // 2, 4), lax.rem(me, 2)
    for dz, dy, dx, dc in ORDER:
        to = lax.rem(z + dz, 2) * 32 + lax.rem(y + dy, 4) * 8 + lax.rem(x + dx, 4) * 2 + lax.rem(core + dc, 2)
        pltpu.make_async_remote_copy(
            src_ref=pos_ref.at[:, to],
            dst_ref=slots.at[me],
            send_sem=send_sem.at[0],
            recv_sem=recv_sem.at[0],
            device_id={"ka": to},
            device_id_type=MESH,
        ).start()
    row = word_ref.at[mine, pl.ds(0, FRAMES - 1)]
    pltpu.make_async_copy(row, row, recv_sem.at[1]).wait()

    def share_group(i, _):
        to = lax.rem(mine + i, groups)
        pltpu.make_async_remote_copy(
            src_ref=word_ref.at[mine],
            dst_ref=word_ref.at[mine],
            send_sem=send_sem.at[3],
            recv_sem=recv_sem.at[3],
            device_id={"ka": to // 2 * wide + 2 * frame + lax.rem(to, 2)},
            device_id_type=MESH,
        ).start()
        return 0

    lax.fori_loop(1, groups, share_group, 0)
    for fetch in fetches:
        fetch.wait()
    most = slots.at[pl.ds(0, count - 1)]
    pltpu.make_async_copy(most, most, recv_sem.at[0]).wait()
    for f in range(FRAMES):
        stage[f] = slots[plan[3, 8 + f]]

    def hand_on(i, _):
        to = lax.rem(frame + i, FRAMES)
        pltpu.make_async_remote_copy(
            src_ref=stage.at[to],
            dst_ref=x_ref.at[frame],
            send_sem=send_sem.at[2],
            recv_sem=recv_sem.at[2],
            device_id={"ka": base + 2 * to},
            device_id_type=MESH,
        ).start()
        return 0

    lax.fori_loop(1, FRAMES, hand_on, 0)
    x_ref[frame] = stage[frame]
    words = word_ref.at[pl.ds(0, groups - 1)]
    rest = x_ref.at[pl.ds(0, FRAMES - 1)]
    pltpu.make_async_copy(words, words, recv_sem.at[3]).wait()
    pltpu.make_async_copy(most, most, send_sem.at[0]).wait()
    pltpu.make_async_copy(row, row, send_sem.at[1]).wait()
    pltpu.make_async_copy(words, words, send_sem.at[3]).wait()
    pltpu.make_async_copy(rest, rest, recv_sem.at[2]).wait()
    pltpu.make_async_copy(rest, rest, send_sem.at[2]).wait()


def call_spread(plan, k_index, counts, positions):
    hbm = pl.BlockSpec(memory_space=pltpu.HBM)
    vmem = pl.BlockSpec(memory_space=pltpu.VMEM)
    count = lax.axis_size("ka")
    rows = positions.shape[2] // (128 * count)
    lanes = k_index.shape[1]
    small = jnp.pad(k_index, ((0, 1), (0, 0))) + jnp.pad(counts, ((3, 0), (0, lanes - 3))) + jnp.pad(plan[None], ((3, 0), (8, lanes - 16)))
    return pl.pallas_call(
        spread_kernel,
        out_shape=(
            jax.ShapeDtypeStruct((FRAMES, 3, rows, 128), f32),
            jax.ShapeDtypeStruct((count // FRAMES, FRAMES, lanes), jnp.int32),
            jax.ShapeDtypeStruct((1, lanes), jnp.int32),
        ),
        in_specs=[vmem, hbm],
        out_specs=(vmem, vmem, vmem),
        scratch_shapes=[
            pltpu.VMEM((count, 3, rows, 128), f32),
            pltpu.VMEM((FRAMES, 3, rows, 128), f32),
            pltpu.SMEM((4, lanes), jnp.int32),
            pltpu.SemaphoreType.DMA((4,)),
            pltpu.SemaphoreType.DMA((4,)),
            pltpu.SemaphoreType.DMA((2,)),
        ],
        compiler_params=pltpu.CompilerParams(collective_id=0, has_side_effects=True, vmem_limit_bytes=55000 * 1024),
    )(small, positions.reshape(3, count, rows, 128))


def pick_blocks(grid, pick, word_ref, modes, blocks, places):
    lanes = lax.broadcasted_iota(jnp.int32, (8, 128), 1)
    upper = lax.broadcasted_iota(jnp.int32, (8, 128), 0) < 4
    for b, at in zip(blocks, places):
        group, lead = b // (2 * FRAMES) * 2 + lax.rem(b, 2), lax.rem(b // 2, FRAMES)
        found = jnp.zeros((8, 128), f32)
        for j in range(128):
            word = pick[group, lead, j]
            found = jnp.where(lanes == j, pltpu.roll(grid[word >> 8], word & 127, axis=1), found)
        sign = jnp.where((word_ref[group, pl.ds(lead, 1)] & 128) > 0, -1.0, 1.0)
        modes[at] = found * jnp.where(upper, 1.0, sign)


def factors_kernel(scale, grid, word_ref, out_ref, modes, spare, parts, beside, pick, send_sem, recv_sem, own_sem):
    me = lax.axis_index("ka")
    half = lax.axis_index("atoms")
    chips = lax.axis_size("ka") // 2
    chip, core = me // 2, lax.rem(me, 2)
    barrier = pltpu.get_barrier_semaphore()
    fetch = pltpu.make_async_copy(word_ref, pick, own_sem)
    fetch.start()

    def greet(i, _):
        to = 2 * lax.rem(chip + i, chips) + core
        pl.semaphore_signal(barrier, inc=1, device_id={"ka": to, "atoms": 1 - half}, device_id_type=MESH)

        @pl.when(i < chips)
        def _():
            pl.semaphore_signal(barrier, inc=1, device_id={"ka": to, "atoms": half}, device_id_type=MESH)
        return 0

    pl.semaphore_signal(barrier, inc=1, device_id={"ka": 2 * chip + 1 - core}, device_id_type=MESH)
    lax.fori_loop(1, chips + 1, greet, 0)
    fetch.wait()
    slot = half * chips + chip

    def place(i):
        return lax.rem(chip + i + 1, chips)

    def hand_over(g):
        pltpu.make_async_remote_copy(
            src_ref=spare.at[pl.ds(BATCH * g, BATCH)],
            dst_ref=beside.at[pl.ds(BATCH * g, BATCH)],
            send_sem=send_sem.at[0],
            recv_sem=recv_sem.at[0],
            device_id={"ka": 2 * chip + 1 - core},
            device_id_type=MESH,
        ).start()

    def first_half(g, _):
        at = [BATCH * g + u for u in range(BATCH)]
        pick_blocks(grid, pick, word_ref, spare, [2 * place(i) + 1 - core for i in at], at)

        @pl.when(g == 1)
        def _():
            pl.semaphore_wait(barrier, 2 * chips)
            hand_over(0)

        @pl.when(g > 0)
        def _():
            hand_over(g)
        return 0

    lax.fori_loop(0, chips // BATCH, first_half, 0)
    handed = beside.at[pl.ds(0, chips)]

    def send(i):
        to = place(i)
        modes[i] += beside[i]

        def copy(h):
            return pltpu.make_async_remote_copy(
                src_ref=modes.at[i],
                dst_ref=parts.at[slot],
                send_sem=send_sem.at[1],
                recv_sem=recv_sem.at[1],
                device_id={"ka": 2 * to + core, "atoms": h},
                device_id_type=MESH,
            )

        copy(1 - half).start()

        @pl.when(i < chips - 1)
        def _():
            copy(half).start()

    def send_next(i, _):
        send(i)
        return 0

    start = 0
    for size in STRETCHES:
        at = list(range(start, start + size))
        pick_blocks(grid, pick, word_ref, modes, [2 * place(i) + core for i in at], at)
        if start == 0:
            pltpu.make_async_copy(handed, handed, recv_sem.at[0]).wait()
        lax.fori_loop(start, start + size, send_next, 0)
        start += size
    parts[slot] = modes[chips - 1]
    most = parts.at[pl.ds(0, 2 * chips - 1)]
    pltpu.make_async_copy(most, most, recv_sem.at[1]).wait()
    window = []
    for f in range(FRAMES):
        total = None
        for high in range(2 * chips // FRAMES):
            part = parts[high * FRAMES + f]
            total = part if total is None else total + part
        window.append(total)
    upper = lax.broadcasted_iota(jnp.int32, (8, 128), 0) < 4
    crossed = [jnp.where(upper, 1.0, -1.0) * pltpu.roll(w, 4, axis=0) for w in window]
    pairs = ((0, 0), (0, 1), (0, 2), (1, 1), (1, 2), (2, 2))
    for f in range(FRAMES):
        wave = window[0]
        for t in range(1, FRAMES):
            turn = 2 * math.pi * (f * t % FRAMES) / FRAMES
            wave = wave + math.cos(turn) * window[t] + math.sin(turn) * crossed[t]
        for p, (a, b) in enumerate(pairs):
            value = wave[a:a + 1] * wave[b:b + 1] + wave[4 + a:5 + a] * wave[4 + b:5 + b]
            out_ref[p, f:f + 1] = value * scale
    pltpu.make_async_copy(handed, handed, send_sem.at[0]).wait()
    pltpu.make_async_copy(most, most, send_sem.at[1]).wait()


def call_factors(grid, words, total_atoms):
    vmem = pl.BlockSpec(memory_space=pltpu.VMEM)
    count = lax.axis_size("ka")
    lanes = words.shape[2]
    return pl.pallas_call(
        functools.partial(factors_kernel, 1.0 / (FRAMES * total_atoms)),
        out_shape=jax.ShapeDtypeStruct((6, FRAMES, lanes), f32),
        in_specs=[vmem, vmem],
        out_specs=vmem,
        scratch_shapes=[
            pltpu.VMEM((count // 2, 8, lanes), f32),
            pltpu.VMEM((count // 2, 8, lanes), f32),
            pltpu.VMEM((count, 8, lanes), f32),
            pltpu.VMEM((count // 2 + 1, 8, lanes), f32),
            pltpu.SMEM(words.shape, jnp.int32),
            pltpu.SemaphoreType.DMA((2,)),
            pltpu.SemaphoreType.DMA((2,)),
            pltpu.SemaphoreType.DMA,
        ],
        compiler_params=pltpu.CompilerParams(collective_id=1, has_side_effects=True, vmem_limit_bytes=20 * 1024 * 1024),
    )(grid.reshape(13 * LINES, 8, 128), words)


def local(positions, counts, plan, k_index):
    x, words, bounds = call_spread(plan, k_index, counts, positions)
    grid = call_lattice(bounds, x)
    factors = call_factors(grid, words, positions.shape[2] * lax.axis_size("atoms"))
    return jnp.transpose(factors, (1, 0, 2))


def solution(mesh):
    return jax.shard_map(
        local,
        mesh=mesh,
        in_specs=(P("ka", None, "atoms"), P("atoms", None), P(), P(None, "ka")),
        out_specs=P(None, None, "ka"),
        check_vma=False,
    )
```
